32 devices in a mesh: wide: 8 (over z, x), narrow: 4 (over y, core).
Axes of the slice: x: 2, y: 2, z: 4, core: 2. Of those that a mesh axis runs over, the one named last changes fastest.
Arguments:
- fields: bfloat16 [24, 128, 8, 512], P(None, None, 'wide', 'narrow'), may hold values from -6 to 6
- neighbors: int32 [4, 8, 512], P(None, 'wide', 'narrow'), may hold values from 0 to 511, as said below
- cost: int32 [8, 512], P('wide', 'narrow'), may hold values from 1 to 8
- dest: int32 [8, 512], P('wide', 'narrow'), may hold values from 0 to 31, as said below
- diffusivity: bfloat16 [128, 8, 512], P(None, 'wide', 'narrow'), may hold values from 0.099609375 to 1
- operators: bfloat16 [8, 128, 128], replicated
Outputs:
- new_fields: bfloat16 [24, 128, 8, 512], P(None, None, 'wide', 'narrow')
- column_burden: float32 [32, 24, 128], P(('wide', 'narrow'))
The draws below stay inside these ranges and needn't reach their ends.
Inputs may be any that keep to these rules, and one draw needn't show every extreme that they name: neighbors[k, r, c] lies within 2 columns of c along the row, counted cyclically over 512, and is never c. `dest`: stretch w * (narrow devices) + n is the device at index w of wide and n of narrow. Of the columns of one device, at most 8 go to one stretch, and exactly 8 go to some stretches; every stretch receives exactly 128 columns in all. Each device deals its columns, in order of rising cost, to its stretches in turn, so that the stretches' summed costs are nearly even while the grid blocks' are not.
All inputs are finite; a program needn't handle non-finite values.
Results may differ from the reference program's by a relative error of at most 0.0068.
Values may be sent and summed in bfloat16 or wider, within the bound.
A program may use at most 64 MiB of HBM per device.

```python
import math
import jax
import jax.numpy as jnp
import numpy as np
from jax import lax

LEVELS = 128
TRACERS = 24
RD = 1
CD = 128
REACH = 2
NEIGH = 4
KMAX = 8
STRETCHES = 32
NCD = 128
CAP = 8
NR = 8
NC = 512


def to_grid(values):
    wide_n = NR // RD
    narrow_n = NC // CD
    return values.reshape(wide_n, narrow_n, RD, CD).transpose(0, 2, 1, 3).reshape(NR, NC).astype(jnp.int32)


def plan_columns(key):
    base = jax.random.fold_in(key, 11)
    key_ceil, key_cost, key_pos, key_shift, key_tie = jax.random.split(base, 5)
    ceilings = 1 + jax.random.permutation(key_ceil, STRETCHES) % KMAX
    costs = jax.random.randint(key_cost, (STRETCHES, NCD), 1, ceilings[:, None] + 1)
    picked = jax.random.randint(key_pos, (STRETCHES, 1), 0, NCD)
    place = jnp.arange(NCD, dtype=jnp.int32)[None, :]
    costs = jnp.where(place == picked, ceilings[:, None], costs)
    tie_keys = jax.random.split(key_tie, STRETCHES)
    ties = jax.vmap(lambda one_key: jax.random.permutation(one_key, NCD))(tie_keys)
    order = jnp.argsort(costs * NCD + ties, axis=1)
    key_rank, key_mix = jax.random.split(key_shift)
    values_all = jnp.arange(STRETCHES, dtype=jnp.int32)
    special = (values_all == 1) | (values_all == STRETCHES - 1) | (values_all == STRETCHES // 2)
    ranks = jax.random.permutation(key_rank, STRETCHES).astype(jnp.int32)
    score = ranks + STRETCHES * (1 - special.astype(jnp.int32))
    chosen = jnp.argsort(score)[:3 * STRETCHES // 4].astype(jnp.int32)
    shifts = chosen[jax.random.permutation(key_mix, 3 * STRETCHES // 4)]
    counts = [CAP] * (STRETCHES // 4) + [CAP // 2] * (STRETCHES // 2)
    sequence = []
    for round_index in range(CAP):
        for shift_index in range(len(counts)):
            if counts[shift_index] > round_index:
                sequence.append(shift_index)
    per_rank = shifts[np.array(sequence, dtype=np.int32)]
    sources = jnp.arange(STRETCHES, dtype=jnp.int32)[:, None]
    values = (sources + per_rank[None, :]) % STRETCHES
    placed = jax.vmap(lambda one_order, one_value: jnp.zeros((NCD,), jnp.int32).at[one_order].set(one_value))(order, values)
    return (costs, placed)


def draw_neighbors(key, part):
    picked = jax.random.randint(key, (NEIGH, NR, NC), 0, 2 * REACH)
    offset = picked - REACH
    offset = offset + (offset >= 0).astype(jnp.int32)
    column = jnp.arange(NC, dtype=jnp.int32)[None, None, :]
    return ((column + offset) % NC).astype(jnp.int32)


def draw_cost(key, part):
    costs, placed = plan_columns(key)
    return to_grid(costs)


def draw_dest(key, part):
    costs, placed = plan_columns(key)
    return to_grid(placed)


def draw_operators(key, part):
    key_diag, key_off = jax.random.split(jax.random.fold_in(key, 23))
    diagonal = jax.random.uniform(key_diag, (KMAX, LEVELS), jnp.float32, 0.4, 0.9)
    offdiag = jax.random.normal(key_off, (KMAX, LEVELS, LEVELS), jnp.float32) * (0.3 / math.sqrt(LEVELS))
    identity = jnp.eye(LEVELS, dtype=jnp.float32)
    return (offdiag * (1.0 - identity) + diagonal[..., :, None] * identity).astype(jnp.bfloat16)


def steps_of(rng, dims, cuts, smallest, top_value):
    loudness = 1.0
    for dim, parts in cuts:
        heights = jax.random.uniform(jax.random.fold_in(jax.random.fold_in(rng, 6), dim), (parts,), jnp.float32, smallest / len(cuts), top_value / len(cuts))
        loudness = loudness * jnp.repeat(jnp.exp(heights), dims[dim] // parts).reshape((-1,) + (1,) * (len(dims) - 1 - dim))
    return loudness


def gaussian(rng, shape, scale, most, shards=(), kind=jnp.bfloat16):
    loudness = steps_of(rng, shape, shards, -0.22, 0.18) if shards else 1.0
    drawn = jax.random.normal(rng, shape, jnp.float32) * scale * loudness
    return jnp.minimum(jnp.maximum(drawn, -most), most).astype(kind)


def setup_inputs(seed: int = 0) -> dict:
    streams_of = jax.random.split(jax.random.key(seed), 7)
    fields = gaussian(streams_of[0], (TRACERS, LEVELS, NR, NC), 1.0, 6.0, ((2, 8), (3, 4)))
    neighbors = draw_neighbors(jax.random.fold_in(streams_of[6], 71), 0)
    cost = draw_cost(jax.random.fold_in(streams_of[6], 71), 0)
    dest = draw_dest(jax.random.fold_in(streams_of[6], 71), 0)
    diffusivity = jnp.clip(jnp.exp(math.log(1.0) - 2.306499 * jax.random.uniform(streams_of[4], (LEVELS, NR, NC), jnp.float32) ** steps_of(streams_of[4], (LEVELS, NR, NC), ((1, 8), (2, 4)), -0.2, 0.2)), 0.099609375, 1.0).astype(jnp.bfloat16)
    operators = draw_operators(jax.random.fold_in(streams_of[6], 71), 0)
    return dict(fields=fields, neighbors=neighbors, cost=cost, dest=dest, diffusivity=diffusivity, operators=operators)


mixing_rate = 0.2


def level_laplace(values, axis):
    length = values.shape[axis]
    first = lax.slice_in_dim(values, 0, 1, axis=axis)
    final = lax.slice_in_dim(values, length - 1, length, axis=axis)
    above = jnp.concatenate([first, lax.slice_in_dim(values, 0, length - 1, axis=axis)], axis=axis)
    below = jnp.concatenate([lax.slice_in_dim(values, 1, length, axis=axis), final], axis=axis)
    return above + below - 2.0 * values


def reference(fields, neighbors, cost, dest, diffusivity, operators):
    tracer_n, level_n, row_n, col_n = fields.shape
    column = jnp.arange(col_n, dtype=jnp.int32)
    offset = (neighbors - column[None, None, :] + REACH) % col_n - REACH
    shift_list = [shift_by for shift_by in range(-REACH, REACH + 1) if shift_by != 0]
    weights = [jnp.sum((offset == shift_by).astype(jnp.float32), axis=0) for shift_by in shift_list]

    def dynamics(tracer):
        values = tracer.astype(jnp.float32)
        summed = (1.0 - NEIGH * mixing_rate) * values
        for shift_by, weight in zip(shift_list, weights):
            summed = summed + mixing_rate * weight * jnp.roll(values, -shift_by, axis=2)
        return summed.astype(jnp.bfloat16)

    dyn = lax.map(dynamics, fields)
    total = row_n * col_n
    dyn_flat = dyn.reshape(tracer_n, level_n, total)
    dyn_cols = jnp.moveaxis(dyn_flat, 2, 0)
    coef_cols = diffusivity.reshape(level_n, total).T
    ops = operators.astype(jnp.float32)
    steps_flat = cost.reshape(-1).astype(jnp.float32)
    row_ids = jnp.arange(row_n, dtype=jnp.int32)[:, None]
    col_ids = jnp.arange(col_n, dtype=jnp.int32)[None, :]
    source = (row_ids // RD) * (col_n // CD) + col_ids // CD
    place = (row_ids % RD) * CD + col_ids % CD
    sort_key = dest * total + source * (RD * CD) + place
    order = jnp.argsort(sort_key.reshape(-1)).astype(jnp.int32)
    groups = order.reshape(STRETCHES, -1)

    def stretch_physics(members):
        start = jnp.take(dyn_cols, members, axis=0)
        coefs = jnp.take(coef_cols, members, axis=0).astype(jnp.float32)[:, None, :]
        steps = jnp.take(steps_flat, members)[:, None, None]
        gains = steps / (4.0 * KMAX) * coefs
        start_f = start.astype(jnp.float32)
        current = start
        final = jnp.zeros_like(start_f)
        for step_index in range(KMAX):
            mixed = jnp.einsum("lm,cqm->cql", ops[step_index], current.astype(jnp.float32))
            widened = mixed + gains * level_laplace(mixed, 2)
            count = float(step_index + 1)
            final = jnp.where(steps == count, widened, final)
            current = jnp.where(steps >= count, widened.astype(jnp.bfloat16), current)
        change = final - start_f
        return change.astype(jnp.bfloat16), jnp.sum(change, axis=2).T

    tends, burdens = lax.map(stretch_physics, groups)
    tend_cols = jnp.zeros((total, tracer_n, level_n), jnp.bfloat16).at[order].set(
        tends.reshape(total, tracer_n, level_n))
    tend_all = jnp.moveaxis(tend_cols, 0, 2)

    def combine(pair):
        return (pair[0].astype(jnp.float32) + pair[1].astype(jnp.float32)).astype(jnp.bfloat16)

    result = lax.map(combine, (dyn_flat, tend_all))
    return result.reshape(fields.shape), burdens
```

```python
import functools

import jax
import jax.numpy as jnp
from jax import lax
from jax.experimental import pallas as pl
from jax.experimental.pallas import tpu as pltpu
from jax.sharding import PartitionSpec as P

REACH = 2
EDGES = 2 * REACH
MESH = pl.DeviceIdType.MESH
F32 = jnp.float32
BF16 = jnp.bfloat16
I32 = jnp.int32


def iota(shape, dim):
    return lax.broadcasted_iota(I32, shape, dim)


def ones_at(mask):
    return jnp.where(mask, 1.0, 0.0).astype(F32)


def dot(a, b):
    return jnp.dot(a, b, preferred_element_type=F32)


def dot_nt(a, b):
    return lax.dot_general(a, b, (((1,), (1,)), ((), ())), preferred_element_type=F32)


def dot_tn(a, b):
    return lax.dot_general(a, b, (((0,), (0,)), ((), ())), preferred_element_type=F32)


def three_parts(values):
    high = values.astype(BF16)
    rest = values - high.astype(F32)
    mid = rest.astype(BF16)
    low = (rest - mid.astype(F32)).astype(BF16)
    return high, mid, low


def kernel(
    wide_n, narrow_n, slots,
    x_ref, nb_ref, cost_ref, dest_ref, diff_ref, op_ref,
    new_ref, burden_ref,
    both_ref, dyn_ref, cur_ref, ge_ref, pack_ref, halo_ref, sums_ref, out_slots, in_slots,
    halo_send, halo_recv, slot_send, slot_recv,
):
    tracer_n, level_n, col_n = x_ref.shape
    substep_n = op_ref.shape[0]
    dev_n = wide_n * narrow_n
    row_span = narrow_n * col_n
    wide = lax.axis_index("wide")
    narrow = lax.axis_index("narrow")
    me = wide * narrow_n + narrow
    base = narrow * col_n

    barrier = pltpu.get_barrier_semaphore()

    def greet(i, carry):
        other = lax.rem(me + i, dev_n)
        pl.semaphore_signal(
            barrier, inc=1, device_id=(other // narrow_n, lax.rem(other, narrow_n)), device_id_type=MESH
        )
        return carry

    lax.fori_loop(1, dev_n, greet, 0)

    src = iota((col_n, col_n), 0)
    lane = iota((col_n, col_n), 1)
    k = lane & (EDGES - 1)
    edge_col = jnp.where(k < REACH, k, col_n - EDGES + k)
    pick = src == edge_col
    group = lax.shift_right_logical(lane, 2)
    packed = jnp.zeros((level_n, col_n), F32)
    for q in range(tracer_n):
        packed += dot(x_ref[q], ones_at(pick & (group == q)).astype(BF16))
    pack_ref[...] = packed.astype(BF16)

    pl.semaphore_wait(barrier, dev_n - 1)
    copies = []
    for side, step in ((0, 1), (1, narrow_n - 1)):
        copies.append(
            pltpu.make_async_remote_copy(
                src_ref=pack_ref,
                dst_ref=halo_ref.at[side],
                send_sem=halo_send.at[side],
                recv_sem=halo_recv.at[side],
                device_id=(wide, lax.rem(narrow + step, narrow_n)),
                device_id_type=MESH,
            )
        )
    for copy in copies:
        copy.start()

    rows = iota((level_n, level_n), 0)
    cols = iota((level_n, level_n), 1)
    second = (
        ones_at(cols == jnp.maximum(rows - 1, 0))
        + ones_at(cols == jnp.minimum(rows + 1, level_n - 1))
        - 2.0 * ones_at(cols == rows)
    ).astype(BF16)
    for s in range(substep_n):
        both_ref[s, :level_n, :] = op_ref[s]
        both_ref[s, level_n:, :] = dot(second, op_ref[s]).astype(BF16)
    cost = cost_ref[...]
    ge = diff_ref[...].astype(F32) * (cost.astype(F32) / (4.0 * substep_n))
    ge_ref[:, :col_n] = ge
    ge_ref[:, col_n:] = ge

    near = ones_at(src == lane)
    side_row = iota((col_n, col_n), 0) & (EDGES - 1)
    left_of = jnp.where(
        side_row >= REACH, lax.rem(base + row_span - EDGES + side_row, row_span), -1
    )
    right_of = jnp.where(side_row < REACH, lax.rem(base + col_n + side_row, row_span), -1)
    from_left = jnp.zeros((col_n, col_n), F32)
    from_right = jnp.zeros((col_n, col_n), F32)
    for n in range(nb_ref.shape[0]):
        neighbor = nb_ref[n : n + 1, :]
        near += ones_at(src == neighbor - base)
        from_left += ones_at(left_of == neighbor)
        from_right += ones_at(right_of == neighbor)
    near = near.astype(BF16)
    row_group = lax.shift_right_logical(src, 2)

    for copy in copies:
        copy.wait()
    left = halo_ref[0]
    right = halo_ref[1]
    for q in range(tracer_n):
        mine = row_group == q
        total = (
            dot(x_ref[q], near)
            + dot(left, jnp.where(mine, from_left, 0.0).astype(BF16))
            + dot(right, jnp.where(mine, from_right, 0.0).astype(BF16))
        )
        dyn = (0.2 * total).astype(BF16)
        dyn_ref[q] = dyn
        cur_ref[q // 2, :, (q % 2) * col_n : (q % 2 + 1) * col_n] = dyn.astype(F32)

    cost_two = jnp.concatenate([cost, cost], axis=1)

    def substep(s, carry):
        both = both_ref[s]
        live = cost_two > s
        for p in range(cur_ref.shape[0]):
            now = cur_ref[p]
            mixed = dot(both, now.astype(BF16))
            moved = mixed[:level_n] + ge_ref[...] * mixed[level_n:]
            cur_ref[p] = jnp.where(live, moved, now)
        return carry

    lax.fori_loop(0, substep_n, substep, 0)

    sums_ref[...] = jnp.ones(sums_ref.shape, F32)
    for q in range(tracer_n):
        change = cur_ref[q // 2, :, (q % 2) * col_n : (q % 2 + 1) * col_n] - dyn_ref[q].astype(F32)
        sums_ref[q : q + 1, :] = jnp.sum(change, axis=0, keepdims=True)
    dest = dest_ref[...]
    hot = ones_at(iota((dev_n, col_n), 0) == dest)
    earlier = dot(hot.astype(BF16), ones_at(src < lane).astype(BF16))
    placed = jnp.sum(hot * earlier, axis=0, keepdims=True).astype(I32)
    spot = ones_at(iota((dev_n * slots, col_n), 0) == dest * slots + placed).astype(BF16)
    filled = jnp.zeros((dev_n * slots, col_n), F32)
    for part in three_parts(sums_ref[...]):
        filled += dot_nt(spot, part)
    filled = filled.reshape(dev_n, slots, col_n)
    out_slots[...] = filled
    in_slots[me] = out_slots[me]

    def send(i, carry):
        other = lax.rem(me + i, dev_n)
        pltpu.make_async_remote_copy(
            src_ref=out_slots.at[other],
            dst_ref=in_slots.at[me],
            send_sem=slot_send,
            recv_sem=slot_recv,
            device_id=(other // narrow_n, lax.rem(other, narrow_n)),
            device_id_type=MESH,
        ).start()
        return carry

    lax.fori_loop(1, dev_n, send, 0)

    for q in range(tracer_n):
        dyn = dyn_ref[q].astype(F32)
        change = cur_ref[q // 2, :, (q % 2) * col_n : (q % 2 + 1) * col_n] - dyn
        new_ref[q] = (dyn + change.astype(BF16).astype(F32)).astype(BF16)

    slot_n = dev_n * slots
    before = ones_at(iota((slot_n, slot_n), 1) < iota((slot_n, slot_n), 0)).astype(BF16)

    others = pl.ds(0, dev_n - 1)
    pltpu.make_async_copy(in_slots.at[others], in_slots.at[others], slot_recv).wait()
    pltpu.make_async_copy(out_slots.at[others], out_slots.at[others], slot_send).wait()
    got = in_slots[...].reshape(slot_n, col_n)
    valid = jnp.broadcast_to(got[:, col_n - 1 :], (slot_n, col_n))
    rank = dot(before, valid.astype(BF16))
    chosen = jnp.where(rank == iota((slot_n, col_n), 1).astype(F32), valid, 0.0).astype(BF16)
    total = jnp.zeros((col_n, col_n), F32)
    for part in three_parts(got):
        total += dot_tn(part, chosen)
    burden_ref[...] = total[:tracer_n]


def local(mesh_shape, fields, neighbors, cost, dest, diffusivity, operators):
    tracer_n, level_n, row_n, col_n = fields.shape
    substep_n = operators.shape[0]
    wide_n, narrow_n = mesh_shape
    dev_n = wide_n * narrow_n
    assert row_n == 1 and tracer_n % 2 == 0 and tracer_n * EDGES <= col_n
    slots = -(-(2 * col_n // dev_n) // 8) * 8
    vmem = pl.BlockSpec(memory_space=pltpu.VMEM)
    new, burden = pl.pallas_call(
        functools.partial(kernel, wide_n, narrow_n, slots),
        out_shape=(
            jax.ShapeDtypeStruct((tracer_n, level_n, col_n), BF16),
            jax.ShapeDtypeStruct((tracer_n, col_n), F32),
        ),
        in_specs=[vmem] * 6,
        out_specs=(vmem, vmem),
        scratch_shapes=[
            pltpu.VMEM((substep_n, 2 * level_n, level_n), BF16),
            pltpu.VMEM((tracer_n, level_n, col_n), BF16),
            pltpu.VMEM((tracer_n // 2, level_n, 2 * col_n), F32),
            pltpu.VMEM((level_n, 2 * col_n), F32),
            pltpu.VMEM((level_n, col_n), BF16),
            pltpu.VMEM((2, level_n, col_n), BF16),
            pltpu.VMEM((col_n, col_n), F32),
            pltpu.VMEM((dev_n, slots, col_n), F32),
            pltpu.VMEM((dev_n, slots, col_n), F32),
            pltpu.SemaphoreType.DMA((2,)),
            pltpu.SemaphoreType.DMA((2,)),
            pltpu.SemaphoreType.DMA,
            pltpu.SemaphoreType.DMA,
        ],
        compiler_params=pltpu.CompilerParams(
            collective_id=0, has_side_effects=True, vmem_limit_bytes=40 * 1024 * 1024
        ),
    )(
        fields.reshape(tracer_n, level_n, col_n),
        neighbors.reshape(neighbors.shape[0], col_n),
        cost,
        dest,
        diffusivity.reshape(level_n, col_n),
        operators,
    )
    return new.reshape(fields.shape), burden[None]


def solution(mesh):
    in_specs = (
        P(None, None, "wide", "narrow"),
        P(None, "wide", "narrow"),
        P("wide", "narrow"),
        P("wide", "narrow"),
        P(None, "wide", "narrow"),
        P(),
    )
    out_specs = (P(None, None, "wide", "narrow"), P(("wide", "narrow"), None, None))
    mesh_shape = (mesh.shape["wide"], mesh.shape["narrow"])
    return jax.shard_map(
        functools.partial(local, mesh_shape),
        mesh=mesh,
        in_specs=in_specs,
        out_specs=out_specs,
        check_vma=False,
    )
```

```python
import functools

import jax
import jax.numpy as jnp
from jax import lax
from jax.experimental import pallas as pl
from jax.experimental.pallas import tpu as pltpu
from jax.sharding import PartitionSpec as P

REACH = 2
EDGES = 2 * REACH
MESH = pl.DeviceIdType.MESH
F32 = jnp.float32
BF16 = jnp.bfloat16
I32 = jnp.int32


def iota(shape, dim):
    return lax.broadcasted_iota(I32, shape, dim)


def ones_at(mask):
    return jnp.where(mask, 1.0, 0.0).astype(F32)


def dot(a, b):
    return jnp.dot(a, b, preferred_element_type=F32)


def dot_nt(a, b):
    return lax.dot_general(a, b, (((1,), (1,)), ((), ())), preferred_element_type=F32)


def dot_tn(a, b):
    return lax.dot_general(a, b, (((0,), (0,)), ((), ())), preferred_element_type=F32)


def wrap(index, size):
    return jnp.where(index >= size, index - size, index)


def kernel(
    wide_n, narrow_n, slots, group_n,
    x_hbm, nb_hbm, cost_hbm, dest_hbm, diff_hbm, op_hbm,
    new_ref, got_ref,
    x_ref, nb_ref, cost_ref, dest_ref, diff_ref, op_ref,
    both_ref, dyn_ref, cur_ref, ge_ref, pack_ref, halo_ref,
    edge_ge, edge_sum, edge_dyn, edge_cur, spot_ref, sums_ref, out_slots, in_slots,
    in_sem, x_sem, halo_send, halo_recv, slot_send, slot_recv,
):
    tracer_n, level_n, col_n = x_ref.shape
    substep_n = op_ref.shape[0]
    dev_n = wide_n * narrow_n
    row_span = narrow_n * col_n
    pair_n = tracer_n // 2
    chunk_n = x_sem.shape[0]
    chunk = tracer_n // chunk_n
    wide = lax.axis_index("wide")
    narrow = lax.axis_index("narrow")
    me = wide * narrow_n + narrow
    base = narrow * col_n

    loads = []
    for index, (far, here) in enumerate(
        ((nb_hbm, nb_ref), (cost_hbm, cost_ref), (dest_hbm, dest_ref), (diff_hbm, diff_ref), (op_hbm, op_ref))
    ):
        loads.append(pltpu.make_async_copy(far, here, in_sem.at[index]))
    x_loads = []
    for index in range(chunk_n):
        part = pl.ds(index * chunk, chunk)
        x_loads.append(pltpu.make_async_copy(x_hbm.at[part], x_ref.at[part], x_sem.at[index]))
    for load in loads[:1] + x_loads + loads[1:]:
        load.start()

    partners = []
    for dw in range(wide_n):
        for dn in range(narrow_n):
            if dw or dn:
                partners.append((wrap(wide + dw, wide_n), wrap(narrow + dn, narrow_n)))
    barrier = pltpu.get_barrier_semaphore()
    for partner in partners:
        pl.semaphore_signal(barrier, inc=1, device_id=partner, device_id_type=MESH)

    src = iota((col_n, col_n), 0)
    lane = iota((col_n, col_n), 1)
    lane_k = lane & (EDGES - 1)
    row_k = src & (EDGES - 1)
    edge_col = jnp.where(lane_k < REACH, col_n - REACH + lane_k, lane_k - REACH)
    pick = ones_at(src == edge_col).astype(BF16)
    shift = EDGES.bit_length() - 1
    lane_q = lax.shift_right_logical(lane, shift)
    row_q = lax.shift_right_logical(src, shift)
    same_q = row_q == lane_q
    left_of = jnp.where(row_k < REACH, lax.rem(base + row_span - REACH + row_k, row_span), -1)
    right_of = jnp.where(row_k >= REACH, lax.rem(base + col_n + row_k - REACH, row_span), -1)

    loads[0].wait()
    near = ones_at(src == lane)
    from_left = jnp.zeros((col_n, col_n), F32)
    from_right = jnp.zeros((col_n, col_n), F32)
    for n in range(nb_ref.shape[0]):
        neighbor = nb_ref[n : n + 1, :]
        near += ones_at(src == neighbor - base)
        from_left += ones_at(left_of == neighbor)
        from_right += ones_at(right_of == neighbor)
    near = near.astype(BF16)

    def edge_shift(q):
        return (EDGES * q + REACH) % col_n

    packed = jnp.zeros((level_n, col_n), F32)
    partial = jnp.zeros((level_n, col_n), F32)
    for q in range(tracer_n):
        if q % chunk == 0:
            x_loads[q // chunk].wait()
        x = x_ref[q]
        total = dot(x, near)
        packed = jnp.where(lane_q == q, pltpu.roll(x.astype(F32), edge_shift(q), 1), packed)
        partial = jnp.where(lane_q == q, pltpu.roll(total, edge_shift(q), 1), partial)
        dyn = (0.2 * total).astype(BF16)
        dyn_ref[q] = dyn
        cur_ref[q // 2, :, (q % 2) * col_n : (q % 2 + 1) * col_n] = dyn.astype(F32)
    pack_ref[...] = packed.astype(BF16)

    pl.semaphore_wait(barrier, dev_n - 1)
    copies = []
    for side, step in ((0, 1), (1, narrow_n - 1)):
        copies.append(
            pltpu.make_async_remote_copy(
                src_ref=pack_ref,
                dst_ref=halo_ref.at[side],
                send_sem=halo_send.at[side],
                recv_sem=halo_recv.at[side],
                device_id=(wide, wrap(narrow + step, narrow_n)),
                device_id_type=MESH,
            )
        )
    for copy in copies:
        copy.start()

    for load in loads[1:]:
        load.wait()
    rows = iota((level_n, level_n), 0)
    cols = iota((level_n, level_n), 1)
    second = (
        ones_at(cols == jnp.maximum(rows - 1, 0))
        + ones_at(cols == jnp.minimum(rows + 1, level_n - 1))
        - 2.0 * ones_at(cols == rows)
    ).astype(BF16)
    for s in range(substep_n):
        both_ref[s, :level_n, :] = op_ref[s]
        both_ref[s, level_n:, :] = dot(second, op_ref[s]).astype(BF16)
    cost = cost_ref[...]
    gain = cost.astype(F32) / (4.0 * substep_n)
    ge = diff_ref[...].astype(F32) * gain
    ge_ref[:, :col_n] = ge
    ge_ref[:, col_n:] = ge

    edge_cost = dot(jnp.broadcast_to(cost.astype(F32), (16, col_n)).astype(BF16), pick)[:1]
    edge_ge[...] = dot(diff_ref[...], pick) * (edge_cost / (4.0 * substep_n))
    edge_sum[...] = partial
    edge_left = jnp.where(same_q, dot(from_left.astype(BF16), pick), 0.0).astype(BF16)
    edge_right = jnp.where(same_q, dot(from_right.astype(BF16), pick), 0.0).astype(BF16)

    dest = dest_ref[...]
    hot = ones_at(iota((dev_n, col_n), 0) == dest)
    earlier = dot(hot.astype(BF16), ones_at(src < lane).astype(BF16))
    placed = jnp.sum(hot * earlier, axis=0, keepdims=True).astype(I32)
    spot_ref[...] = ones_at(iota((slots * dev_n, col_n), 0) == placed * dev_n + dest).astype(BF16)

    cost_two = jnp.concatenate([cost, cost], axis=1)

    def advance(s, pairs):
        both = both_ref[s]
        live = cost_two > s
        for p in pairs:
            now = cur_ref[p]
            mixed = dot(both, now.astype(BF16))
            moved = mixed[:level_n] + ge_ref[...] * mixed[level_n:]
            cur_ref[p] = jnp.where(live, moved, now)

    def leading_half(s, carry):
        advance(s, range(pair_n // 2))
        return carry

    lax.fori_loop(0, substep_n, leading_half, 0, unroll=2)

    for copy in copies:
        copy.wait()
    total = edge_sum[...] + dot(halo_ref[0], edge_left) + dot(halo_ref[1], edge_right)
    start = (0.2 * total).astype(BF16)
    edge_dyn[...] = start
    edge_cur[...] = start.astype(F32)

    def other_half(s, carry):
        advance(s, range(pair_n // 2, pair_n))
        now = edge_cur[...]
        mixed = dot(both_ref[s], now.astype(BF16))
        moved = mixed[:level_n] + edge_ge[...] * mixed[level_n:]
        edge_cur[...] = jnp.where(edge_cost > s.astype(F32), moved, now)
        return carry

    lax.fori_loop(0, substep_n, other_half, 0, unroll=2)

    edge_start = edge_dyn[...].astype(F32)
    edge_change = edge_cur[...] - edge_start
    edge_burden = jnp.broadcast_to(jnp.sum(edge_change, axis=0, keepdims=True), (8, col_n))
    col = iota((1, col_n), 1)
    inner = (col >= REACH) & (col < col_n - REACH)
    sums_ref[...] = jnp.ones(sums_ref.shape, F32)
    for q in range(tracer_n):
        change = cur_ref[q // 2, :, (q % 2) * col_n : (q % 2 + 1) * col_n] - dyn_ref[q].astype(F32)
        outer = pltpu.roll(edge_burden, col_n - edge_shift(q), 1)[:1]
        sums_ref[q : q + 1, :] = jnp.where(inner, jnp.sum(change, axis=0, keepdims=True), outer)
    per_row = col_n // group_n
    sums = sums_ref[...]
    sums = jnp.concatenate([sums] * per_row, axis=0)
    high = sums.astype(BF16)
    low = (sums - high.astype(F32)).astype(BF16)
    filled = dot_nt(spot_ref[...], high) + dot_nt(spot_ref[...], low)
    lane_group = iota((dev_n, col_n), 1) // group_n
    lines = []
    for begin in range(0, slots, per_row):
        line = jnp.zeros((dev_n, col_n), F32)
        for m in range(min(per_row, slots - begin)):
            line = jnp.where(lane_group == m, filled[(begin + m) * dev_n : (begin + m + 1) * dev_n], line)
        lines.append(line)
    line = jnp.concatenate(lines, axis=1)
    for h in range(dev_n):
        out_slots[h] = line[h : h + 1]
    in_slots[me] = out_slots[me]
    for far_wide, far_narrow in partners:
        pltpu.make_async_remote_copy(
            src_ref=out_slots.at[far_wide * narrow_n + far_narrow],
            dst_ref=in_slots.at[me],
            send_sem=slot_send,
            recv_sem=slot_recv,
            device_id=(far_wide, far_narrow),
            device_id_type=MESH,
        ).start()

    edge_new = edge_start + edge_change.astype(BF16).astype(F32)
    for q in range(tracer_n):
        dyn = dyn_ref[q].astype(F32)
        change = cur_ref[q // 2, :, (q % 2) * col_n : (q % 2 + 1) * col_n] - dyn
        new = dyn + change.astype(BF16).astype(F32)
        outer = pltpu.roll(edge_new, col_n - edge_shift(q), 1)
        new_ref[q] = jnp.where(inner, new, outer).astype(BF16)

    others = pl.ds(0, dev_n - 1)
    pltpu.make_async_copy(in_slots.at[others], in_slots.at[others], slot_recv).wait()
    pltpu.make_async_copy(out_slots.at[others], out_slots.at[others], slot_send).wait()
    for h in range(dev_n):
        got_ref[h : h + 1, :] = in_slots[h]


def finish(slots, group_n, tracer_n, new_ref, got_ref, new_hbm, burden_hbm, burden_ref, sem):
    dev_n = got_ref.shape[0]
    col_n = burden_ref.shape[1]
    copy = pltpu.make_async_copy(new_ref, new_hbm, sem.at[0])
    copy.start()
    got = got_ref[...]
    width = got.shape[1]
    per_row = col_n // group_n
    flag = jnp.where(lax.rem(iota(got.shape, 1), group_n) == tracer_n, got, 0.0).astype(BF16)
    count = dot(flag, jnp.ones((width, col_n), BF16))
    before = ones_at(iota((dev_n, dev_n), 1) < iota((dev_n, dev_n), 0)).astype(BF16)
    rank = iota((dev_n, col_n), 1).astype(F32) - dot(before, count.astype(BF16))
    high = got.astype(BF16)
    low = (got - high.astype(F32)).astype(BF16)
    total = jnp.zeros((tracer_n, col_n), F32)
    for row, begin in enumerate(range(0, slots, per_row)):
        members = range(begin, min(begin + per_row, slots))
        chosen = jnp.concatenate(
            [ones_at((rank == float(k)) & (count > float(k))).astype(BF16) for k in members], axis=1
        )
        span = slice(row * col_n, (row + 1) * col_n)
        placed = dot_tn(high[:, span], chosen) + dot_tn(low[:, span], chosen)
        for m in range(len(members)):
            total += placed[m * group_n : m * group_n + tracer_n, m * col_n : (m + 1) * col_n]
    burden_ref[...] = total
    second = pltpu.make_async_copy(burden_ref, burden_hbm, sem.at[1])
    second.start()
    second.wait()
    copy.wait()


def local(mesh_shape, fields, neighbors, cost, dest, diffusivity, operators):
    tracer_n, level_n, row_n, col_n = fields.shape
    substep_n = operators.shape[0]
    neighbor_n = neighbors.shape[0]
    wide_n, narrow_n = mesh_shape
    dev_n = wide_n * narrow_n
    group_n = 1 << tracer_n.bit_length()
    slots = 2 * col_n // dev_n
    assert row_n == 1 and tracer_n % 4 == 0 and tracer_n * EDGES <= col_n and group_n <= col_n
    width = -(-slots * group_n // col_n) * col_n
    hbm = pl.BlockSpec(memory_space=pltpu.HBM)
    vmem = pl.BlockSpec(memory_space=pltpu.VMEM)
    chunk_n = 4
    operands = (
        fields.reshape(tracer_n, level_n, col_n),
        neighbors.reshape(neighbor_n, col_n),
        cost,
        dest,
        diffusivity.reshape(level_n, col_n),
        operators,
    )
    new, got = pl.pallas_call(
        functools.partial(kernel, wide_n, narrow_n, slots, group_n),
        out_shape=(
            jax.ShapeDtypeStruct((tracer_n, level_n, col_n), BF16),
            jax.ShapeDtypeStruct((dev_n, width), F32),
        ),
        in_specs=[hbm] * 6,
        out_specs=(vmem, vmem),
        scratch_shapes=[
            pltpu.VMEM((tracer_n, level_n, col_n), BF16),
            pltpu.VMEM((neighbor_n, col_n), I32),
            pltpu.VMEM((1, col_n), I32),
            pltpu.VMEM((1, col_n), I32),
            pltpu.VMEM((level_n, col_n), BF16),
            pltpu.VMEM((substep_n, level_n, level_n), BF16),
            pltpu.VMEM((substep_n, 2 * level_n, level_n), BF16),
            pltpu.VMEM((tracer_n, level_n, col_n), BF16),
            pltpu.VMEM((tracer_n // 2, level_n, 2 * col_n), F32),
            pltpu.VMEM((level_n, 2 * col_n), F32),
            pltpu.VMEM((level_n, col_n), BF16),
            pltpu.VMEM((2, level_n, col_n), BF16),
            pltpu.VMEM((level_n, col_n), F32),
            pltpu.VMEM((level_n, col_n), F32),
            pltpu.VMEM((level_n, col_n), BF16),
            pltpu.VMEM((level_n, col_n), F32),
            pltpu.VMEM((slots * dev_n, col_n), BF16),
            pltpu.VMEM((group_n, col_n), F32),
            pltpu.VMEM((dev_n, 1, width), F32),
            pltpu.VMEM((dev_n, 1, width), F32),
            pltpu.SemaphoreType.DMA((5,)),
            pltpu.SemaphoreType.DMA((chunk_n,)),
            pltpu.SemaphoreType.DMA((2,)),
            pltpu.SemaphoreType.DMA((2,)),
            pltpu.SemaphoreType.DMA,
            pltpu.SemaphoreType.DMA,
        ],
        compiler_params=pltpu.CompilerParams(
            collective_id=0, has_side_effects=True, vmem_limit_bytes=40 * 1024 * 1024
        ),
    )(*[pltpu.with_memory_space_constraint(value, pltpu.HBM) for value in operands])
    new, burden = pl.pallas_call(
        functools.partial(finish, slots, group_n, tracer_n),
        out_shape=(
            jax.ShapeDtypeStruct((tracer_n, level_n, col_n), BF16),
            jax.ShapeDtypeStruct((tracer_n, col_n), F32),
        ),
        in_specs=[vmem, vmem],
        out_specs=(hbm, hbm),
        scratch_shapes=[pltpu.VMEM((tracer_n, col_n), F32), pltpu.SemaphoreType.DMA((2,))],
    )(new, got)
    return new.reshape(fields.shape), burden[None]


def solution(mesh):
    in_specs = (
        P(None, None, "wide", "narrow"),
        P(None, "wide", "narrow"),
        P("wide", "narrow"),
        P("wide", "narrow"),
        P(None, "wide", "narrow"),
        P(),
    )
    out_specs = (P(None, None, "wide", "narrow"), P(("wide", "narrow"), None, None))
    mesh_shape = (mesh.shape["wide"], mesh.shape["narrow"])
    return jax.shard_map(
        functools.partial(local, mesh_shape),
        mesh=mesh,
        in_specs=in_specs,
        out_specs=out_specs,
        check_vma=False,
    )
```

```python
import functools

import jax
import jax.numpy as jnp
from jax import lax
from jax.experimental import pallas as pl
from jax.experimental.pallas import tpu as pltpu
from jax.sharding import PartitionSpec as P

REACH = 2
EDGES = 2 * REACH
LAG = 2
MESH = pl.DeviceIdType.MESH
F32 = jnp.float32
BF16 = jnp.bfloat16
I32 = jnp.int32


def iota(shape, dim):
    return lax.broadcasted_iota(I32, shape, dim)


def ones_at(mask):
    return jnp.where(mask, 1.0, 0.0).astype(F32)


def dot(a, b):
    return jnp.dot(a, b, preferred_element_type=F32)


def dot_nt(a, b):
    return lax.dot_general(a, b, (((1,), (1,)), ((), ())), preferred_element_type=F32)


def dot_tn(a, b):
    return lax.dot_general(a, b, (((0,), (0,)), ((), ())), preferred_element_type=F32)


def wrap(index, size):
    return jnp.where(index >= size, index - size, index)


def kernel(
    wide_n, narrow_n, slots, group_n,
    x_hbm, nb_hbm, cost_hbm, dest_hbm, diff_hbm, op_hbm,
    new_ref, got_ref,
    x_ref, nb_ref, cost_ref, dest_ref, diff_ref, op_ref,
    both_ref, dyn_ref, cur_ref, ge_ref, pack_ref, halo_ref,
    edge_ge, edge_sum, edge_dyn, edge_cur, spot_ref, sums_ref, out_slots, in_slots,
    in_sem, x_sem, halo_send, halo_recv, slot_send, slot_recv,
):
    tracer_n, level_n, col_n = x_ref.shape
    substep_n = op_ref.shape[0]
    dev_n = wide_n * narrow_n
    row_span = narrow_n * col_n
    pair_n = tracer_n // 2
    chunk_n = x_sem.shape[0]
    chunk = tracer_n // chunk_n
    wide = lax.axis_index("wide")
    narrow = lax.axis_index("narrow")
    me = wide * narrow_n + narrow
    base = narrow * col_n

    loads = []
    for index, (far, here) in enumerate(
        ((nb_hbm, nb_ref), (cost_hbm, cost_ref), (dest_hbm, dest_ref), (diff_hbm, diff_ref), (op_hbm, op_ref))
    ):
        loads.append(pltpu.make_async_copy(far, here, in_sem.at[index]))
    x_loads = []
    for index in range(chunk_n):
        part = pl.ds(index * chunk, chunk)
        x_loads.append(pltpu.make_async_copy(x_hbm.at[part], x_ref.at[part], x_sem.at[index]))
    for load in loads[:1] + x_loads + loads[1:]:
        load.start()

    partners = []
    for dw in range(wide_n):
        for dn in range(narrow_n):
            if dw or dn:
                partners.append((wrap(wide + dw, wide_n), wrap(narrow + dn, narrow_n)))
    barrier = pltpu.get_barrier_semaphore()
    for partner in partners:
        pl.semaphore_signal(barrier, inc=1, device_id=partner, device_id_type=MESH)

    src = iota((col_n, col_n), 0)
    lane = iota((col_n, col_n), 1)
    lane_k = lane & (EDGES - 1)
    row_k = src & (EDGES - 1)
    edge_col = jnp.where(lane_k < REACH, col_n - REACH + lane_k, lane_k - REACH)
    pick = ones_at(src == edge_col).astype(BF16)
    shift = EDGES.bit_length() - 1
    lane_q = lax.shift_right_logical(lane, shift)
    row_q = lax.shift_right_logical(src, shift)
    same_q = row_q == lane_q
    left_of = jnp.where(row_k < REACH, lax.rem(base + row_span - REACH + row_k, row_span), -1)
    right_of = jnp.where(row_k >= REACH, lax.rem(base + col_n + row_k - REACH, row_span), -1)

    loads[0].wait()
    near = ones_at(src == lane)
    from_left = jnp.zeros((col_n, col_n), F32)
    from_right = jnp.zeros((col_n, col_n), F32)
    for n in range(nb_ref.shape[0]):
        neighbor = nb_ref[n : n + 1, :]
        near += ones_at(src == neighbor - base)
        from_left += ones_at(left_of == neighbor)
        from_right += ones_at(right_of == neighbor)
    near = near.astype(BF16)

    def edge_shift(q):
        return (EDGES * q + REACH) % col_n

    packed = jnp.zeros((level_n, col_n), F32)
    partial = jnp.zeros((level_n, col_n), F32)
    for q in range(tracer_n):
        if q % chunk == 0:
            x_loads[q // chunk].wait()
        x = x_ref[q]
        total = dot(x, near)
        packed = jnp.where(lane_q == q, pltpu.roll(x.astype(F32), edge_shift(q), 1), packed)
        partial = jnp.where(lane_q == q, pltpu.roll(total, edge_shift(q), 1), partial)
        dyn = (0.2 * total).astype(BF16)
        dyn_ref[q] = dyn
        cur_ref[q // 2, :, (q % 2) * col_n : (q % 2 + 1) * col_n] = dyn.astype(F32)
    pack_ref[...] = packed.astype(BF16)

    pl.semaphore_wait(barrier, dev_n - 1)
    copies = []
    for side, step in ((0, 1), (1, narrow_n - 1)):
        copies.append(
            pltpu.make_async_remote_copy(
                src_ref=pack_ref,
                dst_ref=halo_ref.at[side],
                send_sem=halo_send.at[side],
                recv_sem=halo_recv.at[side],
                device_id=(wide, wrap(narrow + step, narrow_n)),
                device_id_type=MESH,
            )
        )
    for copy in copies:
        copy.start()

    for load in loads[1:]:
        load.wait()
    rows = iota((level_n, level_n), 0)
    cols = iota((level_n, level_n), 1)
    second = (
        ones_at(cols == jnp.maximum(rows - 1, 0))
        + ones_at(cols == jnp.minimum(rows + 1, level_n - 1))
        - 2.0 * ones_at(cols == rows)
    ).astype(BF16)
    for s in range(substep_n):
        both_ref[s, :level_n, :] = op_ref[s]
        both_ref[s, level_n:, :] = dot(second, op_ref[s]).astype(BF16)
    cost = cost_ref[...]
    gain = cost.astype(F32) / (4.0 * substep_n)
    ge = diff_ref[...].astype(F32) * gain
    ge_ref[:, :col_n] = ge
    ge_ref[:, col_n:] = ge

    edge_cost = dot(jnp.broadcast_to(cost.astype(F32), (16, col_n)).astype(BF16), pick)[:1]
    edge_ge[...] = dot(diff_ref[...], pick) * (edge_cost / (4.0 * substep_n))
    edge_sum[...] = partial
    edge_left = jnp.where(same_q, dot(from_left.astype(BF16), pick), 0.0).astype(BF16)
    edge_right = jnp.where(same_q, dot(from_right.astype(BF16), pick), 0.0).astype(BF16)

    dest = dest_ref[...]
    hot = ones_at(iota((dev_n, col_n), 0) == dest)
    earlier = dot(hot.astype(BF16), ones_at(src < lane).astype(BF16))
    placed = jnp.sum(hot * earlier, axis=0, keepdims=True).astype(I32)
    spot_ref[...] = ones_at(iota((slots * dev_n, col_n), 0) == placed * dev_n + dest).astype(BF16)

    cost_two = jnp.concatenate([cost, cost], axis=1)

    def advance(s, pairs):
        both = both_ref[s]
        live = cost_two > s
        for p in pairs:
            now = cur_ref[p]
            mixed = dot(both, now.astype(BF16))
            moved = mixed[:level_n] + ge_ref[...] * mixed[level_n:]
            cur_ref[p] = jnp.where(live, moved, now)

    def advance_edge(s, now):
        mixed = dot(both_ref[s], now.astype(BF16))
        moved = mixed[:level_n] + edge_ge[...] * mixed[level_n:]
        return jnp.where(edge_cost > jnp.asarray(s, F32), moved, now)

    lag = min(LAG, substep_n)

    def leading(s, carry):
        advance(s, range(pair_n))
        return carry

    lax.fori_loop(0, lag, leading, 0)

    for copy in copies:
        copy.wait()
    total = edge_sum[...] + dot(halo_ref[0], edge_left) + dot(halo_ref[1], edge_right)
    start = (0.2 * total).astype(BF16)
    edge_dyn[...] = start
    edge_cur[...] = start.astype(F32)

    def together(s, carry):
        advance(s, range(pair_n))
        edge_cur[...] = advance_edge(s - lag, edge_cur[...])
        return carry

    lax.fori_loop(lag, substep_n, together, 0)

    edge_end = edge_cur[...]
    for s in range(substep_n - lag, substep_n):
        edge_end = advance_edge(s, edge_end)

    col = iota((1, col_n), 1)
    inner = (col >= REACH) & (col < col_n - REACH)
    inner_sums = []
    for q in range(tracer_n):
        change = cur_ref[q // 2, :, (q % 2) * col_n : (q % 2 + 1) * col_n] - dyn_ref[q].astype(F32)
        inner_sums.append(jnp.sum(change, axis=0, keepdims=True))
    edge_start = edge_dyn[...].astype(F32)
    edge_change = edge_end - edge_start
    edge_burden = jnp.broadcast_to(jnp.sum(edge_change, axis=0, keepdims=True), (8, col_n))
    sums_ref[...] = jnp.ones(sums_ref.shape, F32)
    for q in range(tracer_n):
        outer = pltpu.roll(edge_burden, col_n - edge_shift(q), 1)[:1]
        sums_ref[q : q + 1, :] = jnp.where(inner, inner_sums[q], outer)
    per_row = col_n // group_n
    sums = sums_ref[...]
    sums = jnp.concatenate([sums] * per_row, axis=0)
    high = sums.astype(BF16)
    low = (sums - high.astype(F32)).astype(BF16)
    filled = dot_nt(spot_ref[...], high) + dot_nt(spot_ref[...], low)
    lane_group = iota((dev_n, col_n), 1) // group_n
    lines = []
    for begin in range(0, slots, per_row):
        line = jnp.zeros((dev_n, col_n), F32)
        for m in range(min(per_row, slots - begin)):
            line = jnp.where(lane_group == m, filled[(begin + m) * dev_n : (begin + m + 1) * dev_n], line)
        lines.append(line)
    line = jnp.concatenate(lines, axis=1)
    for h in range(dev_n):
        out_slots[h] = line[h : h + 1]
    in_slots[me] = out_slots[me]
    for far_wide, far_narrow in partners:
        pltpu.make_async_remote_copy(
            src_ref=out_slots.at[far_wide * narrow_n + far_narrow],
            dst_ref=in_slots.at[me],
            send_sem=slot_send,
            recv_sem=slot_recv,
            device_id=(far_wide, far_narrow),
            device_id_type=MESH,
        ).start()

    edge_new = edge_start + edge_change.astype(BF16).astype(F32)
    for q in range(tracer_n):
        dyn = dyn_ref[q].astype(F32)
        change = cur_ref[q // 2, :, (q % 2) * col_n : (q % 2 + 1) * col_n] - dyn
        new = dyn + change.astype(BF16).astype(F32)
        outer = pltpu.roll(edge_new, col_n - edge_shift(q), 1)
        new_ref[q] = jnp.where(inner, new, outer).astype(BF16)

    others = pl.ds(0, dev_n - 1)
    pltpu.make_async_copy(in_slots.at[others], in_slots.at[others], slot_recv).wait()
    pltpu.make_async_copy(out_slots.at[others], out_slots.at[others], slot_send).wait()
    for h in range(dev_n):
        got_ref[h : h + 1, :] = in_slots[h]


def finish(slots, group_n, tracer_n, new_ref, got_ref, new_hbm, burden_hbm, burden_ref, sem):
    dev_n = got_ref.shape[0]
    col_n = burden_ref.shape[1]
    parts = sem.shape[0] - 1
    size = tracer_n // parts
    copies = []
    for index in range(parts):
        part = pl.ds(index * size, size)
        copies.append(pltpu.make_async_copy(new_ref.at[part], new_hbm.at[part], sem.at[index]))
    for copy in copies:
        copy.start()
    got = got_ref[...]
    width = got.shape[1]
    per_row = col_n // group_n
    flag = jnp.where(lax.rem(iota(got.shape, 1), group_n) == tracer_n, got, 0.0).astype(BF16)
    count = dot(flag, jnp.ones((width, col_n), BF16))
    before = ones_at(iota((dev_n, dev_n), 1) < iota((dev_n, dev_n), 0)).astype(BF16)
    rank = iota((dev_n, col_n), 1).astype(F32) - dot(before, count.astype(BF16))
    high = got.astype(BF16)
    low = (got - high.astype(F32)).astype(BF16)
    total = jnp.zeros((tracer_n, col_n), F32)
    for row, begin in enumerate(range(0, slots, per_row)):
        members = range(begin, min(begin + per_row, slots))
        chosen = jnp.concatenate(
            [ones_at((rank == float(k)) & (count > float(k))).astype(BF16) for k in members], axis=1
        )
        span = slice(row * col_n, (row + 1) * col_n)
        placed = dot_tn(high[:, span], chosen) + dot_tn(low[:, span], chosen)
        for m in range(len(members)):
            total += placed[m * group_n : m * group_n + tracer_n, m * col_n : (m + 1) * col_n]
    burden_ref[...] = total
    copies.append(pltpu.make_async_copy(burden_ref, burden_hbm, sem.at[parts]))
    copies[-1].start()
    for copy in copies:
        copy.wait()


def local(mesh_shape, fields, neighbors, cost, dest, diffusivity, operators):
    tracer_n, level_n, row_n, col_n = fields.shape
    substep_n = operators.shape[0]
    neighbor_n = neighbors.shape[0]
    wide_n, narrow_n = mesh_shape
    dev_n = wide_n * narrow_n
    group_n = 1 << tracer_n.bit_length()
    slots = 2 * col_n // dev_n
    assert row_n == 1 and tracer_n % 4 == 0 and tracer_n * EDGES <= col_n and group_n <= col_n
    width = -(-slots * group_n // col_n) * col_n
    hbm = pl.BlockSpec(memory_space=pltpu.HBM)
    vmem = pl.BlockSpec(memory_space=pltpu.VMEM)
    chunk_n = 4
    operands = (
        fields.reshape(tracer_n, level_n, col_n),
        neighbors.reshape(neighbor_n, col_n),
        cost,
        dest,
        diffusivity.reshape(level_n, col_n),
        operators,
    )
    new, got = pl.pallas_call(
        functools.partial(kernel, wide_n, narrow_n, slots, group_n),
        out_shape=(
            jax.ShapeDtypeStruct((tracer_n, level_n, col_n), BF16),
            jax.ShapeDtypeStruct((dev_n, width), F32),
        ),
        in_specs=[hbm] * 6,
        out_specs=(vmem, vmem),
        scratch_shapes=[
            pltpu.VMEM((tracer_n, level_n, col_n), BF16),
            pltpu.VMEM((neighbor_n, col_n), I32),
            pltpu.VMEM((1, col_n), I32),
            pltpu.VMEM((1, col_n), I32),
            pltpu.VMEM((level_n, col_n), BF16),
            pltpu.VMEM((substep_n, level_n, level_n), BF16),
            pltpu.VMEM((substep_n, 2 * level_n, level_n), BF16),
            pltpu.VMEM((tracer_n, level_n, col_n), BF16),
            pltpu.VMEM((tracer_n // 2, level_n, 2 * col_n), F32),
            pltpu.VMEM((level_n, 2 * col_n), F32),
            pltpu.VMEM((level_n, col_n), BF16),
            pltpu.VMEM((2, level_n, col_n), BF16),
            pltpu.VMEM((level_n, col_n), F32),
            pltpu.VMEM((level_n, col_n), F32),
            pltpu.VMEM((level_n, col_n), BF16),
            pltpu.VMEM((level_n, col_n), F32),
            pltpu.VMEM((slots * dev_n, col_n), BF16),
            pltpu.VMEM((group_n, col_n), F32),
            pltpu.VMEM((dev_n, 1, width), F32),
            pltpu.VMEM((dev_n, 1, width), F32),
            pltpu.SemaphoreType.DMA((5,)),
            pltpu.SemaphoreType.DMA((chunk_n,)),
            pltpu.SemaphoreType.DMA((2,)),
            pltpu.SemaphoreType.DMA((2,)),
            pltpu.SemaphoreType.DMA,
            pltpu.SemaphoreType.DMA,
        ],
        compiler_params=pltpu.CompilerParams(
            collective_id=0, has_side_effects=True, vmem_limit_bytes=40 * 1024 * 1024
        ),
    )(*[pltpu.with_memory_space_constraint(value, pltpu.HBM) for value in operands])
    new, burden = pl.pallas_call(
        functools.partial(finish, slots, group_n, tracer_n),
        out_shape=(
            jax.ShapeDtypeStruct((tracer_n, level_n, col_n), BF16),
            jax.ShapeDtypeStruct((tracer_n, col_n), F32),
        ),
        in_specs=[vmem, vmem],
        out_specs=(hbm, hbm),
        scratch_shapes=[pltpu.VMEM((tracer_n, col_n), F32), pltpu.SemaphoreType.DMA((chunk_n + 1,))],
    )(*[pltpu.with_memory_space_constraint(value, pltpu.VMEM) for value in (new, got)])
    return new.reshape(fields.shape), burden[None]


def solution(mesh):
    in_specs = (
        P(None, None, "wide", "narrow"),
        P(None, "wide", "narrow"),
        P("wide", "narrow"),
        P("wide", "narrow"),
        P(None, "wide", "narrow"),
        P(),
    )
    out_specs = (P(None, None, "wide", "narrow"), P(("wide", "narrow"), None, None))
    mesh_shape = (mesh.shape["wide"], mesh.shape["narrow"])
    return jax.shard_map(
        functools.partial(local, mesh_shape),
        mesh=mesh,
        in_specs=in_specs,
        out_specs=out_specs,
        check_vma=False,
    )
```

```python
import functools

import jax
import jax.numpy as jnp
from jax import lax
from jax.experimental import pallas as pl
from jax.experimental.pallas import tpu as pltpu
from jax.sharding import PartitionSpec as P

REACH = 2
EDGES = 2 * REACH
BAND = 16
MESH = pl.DeviceIdType.MESH
F32 = jnp.float32
BF16 = jnp.bfloat16
I32 = jnp.int32


def iota(shape, dim):
    return lax.broadcasted_iota(I32, shape, dim)


def ones_at(mask):
    return jnp.where(mask, 1.0, 0.0).astype(F32)


def dot(a, b):
    return jnp.dot(a, b, preferred_element_type=F32)


def dot_nt(a, b):
    return lax.dot_general(a, b, (((1,), (1,)), ((), ())), preferred_element_type=F32)


def dot_tn(a, b):
    return lax.dot_general(a, b, (((0,), (0,)), ((), ())), preferred_element_type=F32)


def wrap(index, size):
    return jnp.where(index >= size, index - size, index)


def kernel(
    wide_n, narrow_n, slots, group_n,
    x_hbm, nb_hbm, cost_hbm, dest_hbm, diff_hbm, op_hbm,
    new_ref, got_ref,
    x_ref, nb_ref, cost_ref, dest_ref, diff_ref, op_ref,
    both_ref, dyn_ref, cur_ref, ge_ref, pack_ref, halo_ref,
    edge_ge, edge_sum, edge_dyn, edge_cur, spot_ref, sums_ref, out_slots, in_slots,
    in_sem, x_sem, halo_send, halo_recv, slot_send, slot_recv,
):
    tracer_n, level_n, col_n = x_ref.shape
    substep_n = op_ref.shape[0]
    dev_n = wide_n * narrow_n
    row_span = narrow_n * col_n
    pair_n = tracer_n // 2
    chunk_n = x_sem.shape[0]
    chunk = tracer_n // chunk_n
    wide = lax.axis_index("wide")
    narrow = lax.axis_index("narrow")
    me = wide * narrow_n + narrow
    base = narrow * col_n

    loads = []
    for index, (far, here) in enumerate(
        ((nb_hbm, nb_ref), (cost_hbm, cost_ref), (dest_hbm, dest_ref), (diff_hbm, diff_ref), (op_hbm, op_ref))
    ):
        loads.append(pltpu.make_async_copy(far, here, in_sem.at[index]))
    x_loads = []
    for index in range(chunk_n):
        part = pl.ds(index * chunk, chunk)
        x_loads.append(pltpu.make_async_copy(x_hbm.at[part], x_ref.at[part], x_sem.at[index]))
    for load in loads[:1] + x_loads + loads[1:]:
        load.start()

    partners = []
    for dw in range(wide_n):
        for dn in range(narrow_n):
            if dw or dn:
                partners.append((wrap(wide + dw, wide_n), wrap(narrow + dn, narrow_n)))
    barrier = pltpu.get_barrier_semaphore()
    for partner in partners:
        pl.semaphore_signal(barrier, inc=1, device_id=partner, device_id_type=MESH)

    src = iota((col_n, col_n), 0)
    lane = iota((col_n, col_n), 1)
    lane_k = lane & (EDGES - 1)
    row_k = src & (EDGES - 1)
    edge_col = jnp.where(lane_k < REACH, col_n - REACH + lane_k, lane_k - REACH)
    pick = ones_at(src == edge_col).astype(BF16)
    shift = EDGES.bit_length() - 1
    lane_q = lax.shift_right_logical(lane, shift)
    row_q = lax.shift_right_logical(src, shift)
    same_q = row_q == lane_q
    left_of = jnp.where(row_k < REACH, lax.rem(base + row_span - REACH + row_k, row_span), -1)
    right_of = jnp.where(row_k >= REACH, lax.rem(base + col_n + row_k - REACH, row_span), -1)

    loads[0].wait()
    near = ones_at(src == lane)
    from_left = jnp.zeros((col_n, col_n), F32)
    from_right = jnp.zeros((col_n, col_n), F32)
    for n in range(nb_ref.shape[0]):
        neighbor = nb_ref[n : n + 1, :]
        near += ones_at(src == neighbor - base)
        from_left += ones_at(left_of == neighbor)
        from_right += ones_at(right_of == neighbor)
    near = near.astype(BF16)

    def edge_shift(q):
        return (EDGES * q + REACH) % col_n

    packed = jnp.zeros((level_n, col_n), F32)
    partial = jnp.zeros((level_n, col_n), F32)
    for q in range(tracer_n):
        if q % chunk == 0:
            x_loads[q // chunk].wait()
        x = x_ref[q]
        total = dot(x, near)
        packed = jnp.where(lane_q == q, pltpu.roll(x.astype(F32), edge_shift(q), 1), packed)
        partial = jnp.where(lane_q == q, pltpu.roll(total, edge_shift(q), 1), partial)
        dyn = (0.2 * total).astype(BF16)
        dyn_ref[q] = dyn
        cur_ref[q // 2, :, (q % 2) * col_n : (q % 2 + 1) * col_n] = dyn.astype(F32)
    pack_ref[...] = packed.astype(BF16)

    pl.semaphore_wait(barrier, dev_n - 1)
    copies = []
    for side, step in ((0, 1), (1, narrow_n - 1)):
        copies.append(
            pltpu.make_async_remote_copy(
                src_ref=pack_ref,
                dst_ref=halo_ref.at[side],
                send_sem=halo_send.at[side],
                recv_sem=halo_recv.at[side],
                device_id=(wide, wrap(narrow + step, narrow_n)),
                device_id_type=MESH,
            )
        )
    for copy in copies:
        copy.start()

    for load in loads[1:]:
        load.wait()
    rows = iota((level_n, level_n), 0)
    cols = iota((level_n, level_n), 1)
    second = (
        ones_at(cols == jnp.maximum(rows - 1, 0))
        + ones_at(cols == jnp.minimum(rows + 1, level_n - 1))
        - 2.0 * ones_at(cols == rows)
    ).astype(BF16)
    for s in range(substep_n):
        curved = dot(second, op_ref[s]).astype(BF16)
        for begin in range(0, level_n, BAND):
            both_ref[s, 2 * begin : 2 * begin + BAND, :] = op_ref[s, begin : begin + BAND, :]
            both_ref[s, 2 * begin + BAND : 2 * begin + 2 * BAND, :] = curved[begin : begin + BAND]
    cost = cost_ref[...]
    gain = cost.astype(F32) / (4.0 * substep_n)
    ge = diff_ref[...].astype(F32) * gain
    ge_ref[:, :col_n] = ge
    ge_ref[:, col_n:] = ge

    edge_cost = dot(jnp.broadcast_to(cost.astype(F32), (16, col_n)).astype(BF16), pick)[:1]
    edge_ge[...] = dot(diff_ref[...], pick) * (edge_cost / (4.0 * substep_n))
    edge_sum[...] = partial
    edge_left = jnp.where(same_q, dot(from_left.astype(BF16), pick), 0.0).astype(BF16)
    edge_right = jnp.where(same_q, dot(from_right.astype(BF16), pick), 0.0).astype(BF16)

    dest = dest_ref[...]
    hot = ones_at(iota((dev_n, col_n), 0) == dest)
    earlier = dot(hot.astype(BF16), ones_at(src < lane).astype(BF16))
    placed = jnp.sum(hot * earlier, axis=0, keepdims=True).astype(I32)
    spot_ref[...] = ones_at(iota((slots * dev_n, col_n), 0) == placed * dev_n + dest).astype(BF16)

    cost_two = jnp.concatenate([cost, cost], axis=1)

    def advance(both, ref, weight_ref, live):
        mixed = dot(both, ref[...].astype(BF16))
        for begin in range(0, level_n, BAND):
            band = slice(begin, begin + BAND)
            moved = mixed[2 * begin : 2 * begin + BAND] + weight_ref[band] * mixed[2 * begin + BAND : 2 * begin + 2 * BAND]
            ref[band] = jnp.where(live, moved, ref[band])

    def advance_pairs(s, pairs):
        both = both_ref[s]
        live = cost_two > s
        for p in pairs:
            advance(both, cur_ref.at[p], ge_ref, live)
        return both

    def leading_half(s, carry):
        advance_pairs(s, range(pair_n // 2))
        return carry

    lax.fori_loop(0, substep_n, leading_half, 0, unroll=2)

    for copy in copies:
        copy.wait()
    total = edge_sum[...] + dot(halo_ref[0], edge_left) + dot(halo_ref[1], edge_right)
    start = (0.2 * total).astype(BF16)
    edge_dyn[...] = start
    edge_cur[...] = start.astype(F32)

    def other_half(s, carry):
        both = advance_pairs(s, range(pair_n // 2, pair_n))
        advance(both, edge_cur, edge_ge, edge_cost > jnp.asarray(s, F32))
        return carry

    lax.fori_loop(0, substep_n, other_half, 0, unroll=2)
    edge_end = edge_cur[...]

    col = iota((1, col_n), 1)
    inner = (col >= REACH) & (col < col_n - REACH)
    inner_sums = []
    for q in range(tracer_n):
        change = cur_ref[q // 2, :, (q % 2) * col_n : (q % 2 + 1) * col_n] - dyn_ref[q].astype(F32)
        inner_sums.append(jnp.sum(change, axis=0, keepdims=True))
    edge_start = edge_dyn[...].astype(F32)
    edge_change = edge_end - edge_start
    edge_burden = jnp.broadcast_to(jnp.sum(edge_change, axis=0, keepdims=True), (8, col_n))
    sums_ref[...] = jnp.ones(sums_ref.shape, F32)
    for q in range(tracer_n):
        outer = pltpu.roll(edge_burden, col_n - edge_shift(q), 1)[:1]
        sums_ref[q : q + 1, :] = jnp.where(inner, inner_sums[q], outer)
    per_row = col_n // group_n
    sums = sums_ref[...]
    sums = jnp.concatenate([sums] * per_row, axis=0)
    high = sums.astype(BF16)
    low = (sums - high.astype(F32)).astype(BF16)
    filled = dot_nt(spot_ref[...], high) + dot_nt(spot_ref[...], low)
    lane_group = iota((dev_n, col_n), 1) // group_n
    lines = []
    for begin in range(0, slots, per_row):
        line = jnp.zeros((dev_n, col_n), F32)
        for m in range(min(per_row, slots - begin)):
            line = jnp.where(lane_group == m, filled[(begin + m) * dev_n : (begin + m + 1) * dev_n], line)
        lines.append(line)
    line = jnp.concatenate(lines, axis=1)
    for h in range(dev_n):
        out_slots[h] = line[h : h + 1]
    in_slots[me] = out_slots[me]
    for far_wide, far_narrow in partners:
        pltpu.make_async_remote_copy(
            src_ref=out_slots.at[far_wide * narrow_n + far_narrow],
            dst_ref=in_slots.at[me],
            send_sem=slot_send,
            recv_sem=slot_recv,
            device_id=(far_wide, far_narrow),
            device_id_type=MESH,
        ).start()

    edge_new = edge_start + edge_change.astype(BF16).astype(F32)
    for q in range(tracer_n):
        dyn = dyn_ref[q].astype(F32)
        change = cur_ref[q // 2, :, (q % 2) * col_n : (q % 2 + 1) * col_n] - dyn
        new = dyn + change.astype(BF16).astype(F32)
        outer = pltpu.roll(edge_new, col_n - edge_shift(q), 1)
        new_ref[q] = jnp.where(inner, new, outer).astype(BF16)

    others = pl.ds(0, dev_n - 1)
    pltpu.make_async_copy(in_slots.at[others], in_slots.at[others], slot_recv).wait()
    pltpu.make_async_copy(out_slots.at[others], out_slots.at[others], slot_send).wait()
    for h in range(dev_n):
        got_ref[h : h + 1, :] = in_slots[h]


def finish(slots, group_n, tracer_n, new_ref, got_ref, new_hbm, burden_hbm, burden_ref, sem):
    dev_n = got_ref.shape[0]
    col_n = burden_ref.shape[1]
    parts = sem.shape[0] - 1
    size = tracer_n // parts
    copies = []
    for index in range(parts):
        part = pl.ds(index * size, size)
        copies.append(pltpu.make_async_copy(new_ref.at[part], new_hbm.at[part], sem.at[index]))
    for copy in copies:
        copy.start()
    got = got_ref[...]
    width = got.shape[1]
    per_row = col_n // group_n
    flag = jnp.where(lax.rem(iota(got.shape, 1), group_n) == tracer_n, got, 0.0).astype(BF16)
    count = dot(flag, jnp.ones((width, col_n), BF16))
    before = ones_at(iota((dev_n, dev_n), 1) < iota((dev_n, dev_n), 0)).astype(BF16)
    rank = iota((dev_n, col_n), 1).astype(F32) - dot(before, count.astype(BF16))
    high = got.astype(BF16)
    low = (got - high.astype(F32)).astype(BF16)
    total = jnp.zeros((tracer_n, col_n), F32)
    for row, begin in enumerate(range(0, slots, per_row)):
        members = range(begin, min(begin + per_row, slots))
        chosen = jnp.concatenate(
            [ones_at((rank == float(k)) & (count > float(k))).astype(BF16) for k in members], axis=1
        )
        span = slice(row * col_n, (row + 1) * col_n)
        placed = dot_tn(high[:, span], chosen) + dot_tn(low[:, span], chosen)
        for m in range(len(members)):
            total += placed[m * group_n : m * group_n + tracer_n, m * col_n : (m + 1) * col_n]
    burden_ref[...] = total
    copies.append(pltpu.make_async_copy(burden_ref, burden_hbm, sem.at[parts]))
    copies[-1].start()
    for copy in copies:
        copy.wait()


def local(mesh_shape, fields, neighbors, cost, dest, diffusivity, operators):
    tracer_n, level_n, row_n, col_n = fields.shape
    substep_n = operators.shape[0]
    neighbor_n = neighbors.shape[0]
    wide_n, narrow_n = mesh_shape
    dev_n = wide_n * narrow_n
    group_n = 1 << tracer_n.bit_length()
    slots = 2 * col_n // dev_n
    assert row_n == 1 and tracer_n % 4 == 0 and level_n % BAND == 0 and tracer_n * EDGES <= col_n and group_n <= col_n
    width = -(-slots * group_n // col_n) * col_n
    hbm = pl.BlockSpec(memory_space=pltpu.HBM)
    vmem = pl.BlockSpec(memory_space=pltpu.VMEM)
    chunk_n = 4
    operands = (
        fields.reshape(tracer_n, level_n, col_n),
        neighbors.reshape(neighbor_n, col_n),
        cost,
        dest,
        diffusivity.reshape(level_n, col_n),
        operators,
    )
    new, got = pl.pallas_call(
        functools.partial(kernel, wide_n, narrow_n, slots, group_n),
        out_shape=(
            jax.ShapeDtypeStruct((tracer_n, level_n, col_n), BF16),
            jax.ShapeDtypeStruct((dev_n, width), F32),
        ),
        in_specs=[hbm] * 6,
        out_specs=(vmem, vmem),
        scratch_shapes=[
            pltpu.VMEM((tracer_n, level_n, col_n), BF16),
            pltpu.VMEM((neighbor_n, col_n), I32),
            pltpu.VMEM((1, col_n), I32),
            pltpu.VMEM((1, col_n), I32),
            pltpu.VMEM((level_n, col_n), BF16),
            pltpu.VMEM((substep_n, level_n, level_n), BF16),
            pltpu.VMEM((substep_n, 2 * level_n, level_n), BF16),
            pltpu.VMEM((tracer_n, level_n, col_n), BF16),
            pltpu.VMEM((tracer_n // 2, level_n, 2 * col_n), F32),
            pltpu.VMEM((level_n, 2 * col_n), F32),
            pltpu.VMEM((level_n, col_n), BF16),
            pltpu.VMEM((2, level_n, col_n), BF16),
            pltpu.VMEM((level_n, col_n), F32),
            pltpu.VMEM((level_n, col_n), F32),
            pltpu.VMEM((level_n, col_n), BF16),
            pltpu.VMEM((level_n, col_n), F32),
            pltpu.VMEM((slots * dev_n, col_n), BF16),
            pltpu.VMEM((group_n, col_n), F32),
            pltpu.VMEM((dev_n, 1, width), F32),
            pltpu.VMEM((dev_n, 1, width), F32),
            pltpu.SemaphoreType.DMA((5,)),
            pltpu.SemaphoreType.DMA((chunk_n,)),
            pltpu.SemaphoreType.DMA((2,)),
            pltpu.SemaphoreType.DMA((2,)),
            pltpu.SemaphoreType.DMA,
            pltpu.SemaphoreType.DMA,
        ],
        compiler_params=pltpu.CompilerParams(
            collective_id=0, has_side_effects=True, vmem_limit_bytes=40 * 1024 * 1024
        ),
    )(*[pltpu.with_memory_space_constraint(value, pltpu.HBM) for value in operands])
    new, burden = pl.pallas_call(
        functools.partial(finish, slots, group_n, tracer_n),
        out_shape=(
            jax.ShapeDtypeStruct((tracer_n, level_n, col_n), BF16),
            jax.ShapeDtypeStruct((tracer_n, col_n), F32),
        ),
        in_specs=[vmem, vmem],
        out_specs=(hbm, hbm),
        scratch_shapes=[pltpu.VMEM((tracer_n, col_n), F32), pltpu.SemaphoreType.DMA((chunk_n + 1,))],
    )(*[pltpu.with_memory_space_constraint(value, pltpu.VMEM) for value in (new, got)])
    return new.reshape(fields.shape), burden[None]


def solution(mesh):
    in_specs = (
        P(None, None, "wide", "narrow"),
        P(None, "wide", "narrow"),
        P("wide", "narrow"),
        P("wide", "narrow"),
        P(None, "wide", "narrow"),
        P(),
    )
    out_specs = (P(None, None, "wide", "narrow"), P(("wide", "narrow"), None, None))
    mesh_shape = (mesh.shape["wide"], mesh.shape["narrow"])
    return jax.shard_map(
        functools.partial(local, mesh_shape),
        mesh=mesh,
        in_specs=in_specs,
        out_specs=out_specs,
        check_vma=False,
    )
```

```python
import functools

import jax
import jax.numpy as jnp
from jax import lax
from jax.experimental import pallas as pl
from jax.experimental.pallas import tpu as pltpu
from jax.sharding import PartitionSpec as P

REACH = 2
EDGES = 2 * REACH
BAND = 16
MESH = pl.DeviceIdType.MESH
F32 = jnp.float32
BF16 = jnp.bfloat16
I32 = jnp.int32


def iota(shape, dim):
    return lax.broadcasted_iota(I32, shape, dim)


def ones_at(mask):
    return jnp.where(mask, 1.0, 0.0).astype(F32)


def dot(a, b):
    return jnp.dot(a, b, preferred_element_type=F32)


def dot_nt(a, b):
    return lax.dot_general(a, b, (((1,), (1,)), ((), ())), preferred_element_type=F32)


def dot_tn(a, b):
    return lax.dot_general(a, b, (((0,), (0,)), ((), ())), preferred_element_type=F32)


def wrap(index, size):
    return jnp.where(index >= size, index - size, index)


def kernel(
    wide_n, narrow_n, slots, group_n,
    x_hbm, nb_hbm, cost_hbm, dest_hbm, diff_hbm, op_hbm,
    new_ref, got_ref,
    x_ref, nb_ref, cost_ref, dest_ref, diff_ref, op_ref,
    both_ref, dyn_ref, cur_ref, ge_ref, pack_ref, halo_ref,
    edge_ge, edge_sum, edge_dyn, edge_cur, spot_ref, sums_ref, out_slots, in_slots,
    in_sem, x_sem, halo_send, halo_recv, slot_send, slot_recv,
):
    tracer_n, level_n, col_n = x_ref.shape
    substep_n = op_ref.shape[0]
    dev_n = wide_n * narrow_n
    row_span = narrow_n * col_n
    pair_n = tracer_n // 2
    chunk_n = x_sem.shape[0]
    chunk = tracer_n // chunk_n
    wide = lax.axis_index("wide")
    narrow = lax.axis_index("narrow")
    me = wide * narrow_n + narrow
    base = narrow * col_n

    loads = []
    for index, (far, here) in enumerate(
        ((nb_hbm, nb_ref), (cost_hbm, cost_ref), (dest_hbm, dest_ref), (diff_hbm, diff_ref), (op_hbm, op_ref))
    ):
        loads.append(pltpu.make_async_copy(far, here, in_sem.at[index]))
    x_loads = []
    for index in range(chunk_n):
        part = pl.ds(index * chunk, chunk)
        x_loads.append(pltpu.make_async_copy(x_hbm.at[part], x_ref.at[part], x_sem.at[index]))
    for load in loads[:1] + x_loads + loads[1:]:
        load.start()

    partners = []
    for dw in range(wide_n):
        for dn in range(narrow_n):
            if dw or dn:
                partners.append((wrap(wide + dw, wide_n), wrap(narrow + dn, narrow_n)))
    barrier = pltpu.get_barrier_semaphore()
    for partner in partners:
        pl.semaphore_signal(barrier, inc=1, device_id=partner, device_id_type=MESH)

    src = iota((col_n, col_n), 0)
    lane = iota((col_n, col_n), 1)
    lane_k = lane & (EDGES - 1)
    row_k = src & (EDGES - 1)
    edge_col = jnp.where(lane_k < REACH, col_n - REACH + lane_k, lane_k - REACH)
    pick = ones_at(src == edge_col).astype(BF16)
    shift = EDGES.bit_length() - 1
    lane_q = lax.shift_right_logical(lane, shift)
    row_q = lax.shift_right_logical(src, shift)
    same_q = row_q == lane_q
    left_of = jnp.where(row_k < REACH, wrap(base + row_span - REACH + row_k, row_span), -1)
    right_of = jnp.where(row_k >= REACH, wrap(base + col_n + row_k - REACH, row_span), -1)

    loads[0].wait()
    near = ones_at(src == lane)
    from_left = jnp.zeros((col_n, col_n), F32)
    from_right = jnp.zeros((col_n, col_n), F32)
    for n in range(nb_ref.shape[0]):
        neighbor = nb_ref[n : n + 1, :]
        near += ones_at(src == neighbor - base)
        from_left += ones_at(left_of == neighbor)
        from_right += ones_at(right_of == neighbor)
    near = near.astype(BF16)

    def edge_shift(q):
        return (EDGES * q + REACH) % col_n

    packed = jnp.zeros((level_n, col_n), F32)
    partial = jnp.zeros((level_n, col_n), F32)
    for q in range(tracer_n):
        if q % chunk == 0:
            x_loads[q // chunk].wait()
        x = x_ref[q]
        total = dot(x, near)
        packed = jnp.where(lane_q == q, pltpu.roll(x.astype(F32), edge_shift(q), 1), packed)
        partial = jnp.where(lane_q == q, pltpu.roll(total, edge_shift(q), 1), partial)
        dyn = (0.2 * total).astype(BF16)
        dyn_ref[q] = dyn
        cur_ref[q // 2, :, (q % 2) * col_n : (q % 2 + 1) * col_n] = dyn.astype(F32)
    pack_ref[...] = packed.astype(BF16)

    pl.semaphore_wait(barrier, dev_n - 1)
    copies = []
    for side, step in ((0, 1), (1, narrow_n - 1)):
        copies.append(
            pltpu.make_async_remote_copy(
                src_ref=pack_ref,
                dst_ref=halo_ref.at[side],
                send_sem=halo_send.at[side],
                recv_sem=halo_recv.at[side],
                device_id=(wide, wrap(narrow + step, narrow_n)),
                device_id_type=MESH,
            )
        )
    for copy in copies:
        copy.start()

    for load in loads[1:]:
        load.wait()
    rows = iota((level_n, level_n), 0)
    cols = iota((level_n, level_n), 1)
    second = (
        ones_at(cols == jnp.maximum(rows - 1, 0))
        + ones_at(cols == jnp.minimum(rows + 1, level_n - 1))
        - 2.0 * ones_at(cols == rows)
    ).astype(BF16)
    for s in range(substep_n):
        curved = dot(second, op_ref[s]).astype(BF16)
        for begin in range(0, level_n, BAND):
            both_ref[s, 2 * begin : 2 * begin + BAND, :] = op_ref[s, begin : begin + BAND, :]
            both_ref[s, 2 * begin + BAND : 2 * begin + 2 * BAND, :] = curved[begin : begin + BAND]
    cost = cost_ref[...]
    gain = cost.astype(F32) / (4.0 * substep_n)
    ge = diff_ref[...].astype(F32) * gain
    ge_ref[:, :col_n] = ge
    ge_ref[:, col_n:] = ge

    edge_cost = dot(jnp.broadcast_to(cost.astype(F32), (16, col_n)).astype(BF16), pick)[:1]
    edge_ge[...] = dot(diff_ref[...], pick) * (edge_cost / (4.0 * substep_n))
    edge_sum[...] = partial
    edge_left = jnp.where(same_q, dot(from_left.astype(BF16), pick), 0.0).astype(BF16)
    edge_right = jnp.where(same_q, dot(from_right.astype(BF16), pick), 0.0).astype(BF16)

    dest = dest_ref[...]
    hot = ones_at(iota((dev_n, col_n), 0) == dest)
    earlier = dot(hot.astype(BF16), ones_at(src < lane).astype(BF16))
    placed = jnp.sum(hot * earlier, axis=0, keepdims=True).astype(I32)
    spot_ref[...] = ones_at(iota((slots * dev_n, col_n), 0) == placed * dev_n + dest).astype(BF16)

    cost_two = jnp.concatenate([cost, cost], axis=1)

    def advance(both, ref, weight_ref, live):
        mixed = dot(both, ref[...].astype(BF16))
        for begin in range(0, level_n, BAND):
            band = slice(begin, begin + BAND)
            moved = mixed[2 * begin : 2 * begin + BAND] + weight_ref[band] * mixed[2 * begin + BAND : 2 * begin + 2 * BAND]
            ref[band] = jnp.where(live, moved, ref[band])

    def advance_pairs(s, pairs):
        both = both_ref[s]
        live = cost_two > s
        for p in pairs:
            advance(both, cur_ref.at[p], ge_ref, live)
        return both

    inner_sums = []

    def add_up(q):
        change = cur_ref[q // 2, :, (q % 2) * col_n : (q % 2 + 1) * col_n] - dyn_ref[q].astype(F32)
        inner_sums.append(jnp.sum(change, axis=0, keepdims=True))

    for s in range(substep_n):
        advance_pairs(s, range(pair_n // 2))

    for copy in copies:
        copy.wait()
    total = edge_sum[...] + dot(halo_ref[0], edge_left) + dot(halo_ref[1], edge_right)
    start = (0.2 * total).astype(BF16)
    edge_dyn[...] = start
    edge_cur[...] = start.astype(F32)

    for s in range(substep_n):
        both = advance_pairs(s, range(pair_n // 2, pair_n))
        advance(both, edge_cur, edge_ge, edge_cost > float(s))
        for q in range(s * pair_n // substep_n, (s + 1) * pair_n // substep_n):
            add_up(q)
    for q in range(pair_n, tracer_n):
        add_up(q)
    edge_end = edge_cur[...]

    col = iota((1, col_n), 1)
    inner = (col >= REACH) & (col < col_n - REACH)
    edge_start = edge_dyn[...].astype(F32)
    edge_change = edge_end - edge_start
    edge_burden = jnp.broadcast_to(jnp.sum(edge_change, axis=0, keepdims=True), (8, col_n))
    sums_ref[...] = jnp.ones(sums_ref.shape, F32)
    for q in range(tracer_n):
        outer = pltpu.roll(edge_burden, col_n - edge_shift(q), 1)[:1]
        sums_ref[q : q + 1, :] = jnp.where(inner, inner_sums[q], outer)
    per_row = col_n // group_n
    sums = sums_ref[...]
    sums = jnp.concatenate([sums] * per_row, axis=0)
    high = sums.astype(BF16)
    low = (sums - high.astype(F32)).astype(BF16)
    filled = dot_nt(spot_ref[...], high) + dot_nt(spot_ref[...], low)
    lane_group = iota((dev_n, col_n), 1) // group_n
    lines = []
    for begin in range(0, slots, per_row):
        line = jnp.zeros((dev_n, col_n), F32)
        for m in range(min(per_row, slots - begin)):
            line = jnp.where(lane_group == m, filled[(begin + m) * dev_n : (begin + m + 1) * dev_n], line)
        lines.append(line)
    line = jnp.concatenate(lines, axis=1)
    for h in range(dev_n):
        out_slots[h] = line[h : h + 1]
    in_slots[me] = out_slots[me]
    for far_wide, far_narrow in partners:
        pltpu.make_async_remote_copy(
            src_ref=out_slots.at[far_wide * narrow_n + far_narrow],
            dst_ref=in_slots.at[me],
            send_sem=slot_send,
            recv_sem=slot_recv,
            device_id=(far_wide, far_narrow),
            device_id_type=MESH,
        ).start()

    edge_new = edge_start + edge_change.astype(BF16).astype(F32)
    for q in range(tracer_n):
        dyn = dyn_ref[q].astype(F32)
        change = cur_ref[q // 2, :, (q % 2) * col_n : (q % 2 + 1) * col_n] - dyn
        new = dyn + change.astype(BF16).astype(F32)
        outer = pltpu.roll(edge_new, col_n - edge_shift(q), 1)
        new_ref[q] = jnp.where(inner, new, outer).astype(BF16)

    others = pl.ds(0, dev_n - 1)
    pltpu.make_async_copy(in_slots.at[others], in_slots.at[others], slot_recv).wait()
    pltpu.make_async_copy(out_slots.at[others], out_slots.at[others], slot_send).wait()
    for h in range(dev_n):
        got_ref[h : h + 1, :] = in_slots[h]


def finish(slots, group_n, tracer_n, new_ref, got_ref, new_hbm, burden_hbm, burden_ref, sem):
    dev_n = got_ref.shape[0]
    col_n = burden_ref.shape[1]
    parts = sem.shape[0] - 1
    size = tracer_n // parts
    copies = []
    for index in range(parts):
        part = pl.ds(index * size, size)
        copies.append(pltpu.make_async_copy(new_ref.at[part], new_hbm.at[part], sem.at[index]))
    for copy in copies:
        copy.start()
    got = got_ref[...]
    width = got.shape[1]
    per_row = col_n // group_n
    flag = jnp.where(lax.rem(iota(got.shape, 1), group_n) == tracer_n, got, 0.0).astype(BF16)
    count = dot(flag, jnp.ones((width, col_n), BF16))
    before = ones_at(iota((dev_n, dev_n), 1) < iota((dev_n, dev_n), 0)).astype(BF16)
    rank = iota((dev_n, col_n), 1).astype(F32) - dot(before, count.astype(BF16))
    high = got.astype(BF16)
    low = (got - high.astype(F32)).astype(BF16)
    total = jnp.zeros((tracer_n, col_n), F32)
    for row, begin in enumerate(range(0, slots, per_row)):
        members = range(begin, min(begin + per_row, slots))
        chosen = jnp.concatenate(
            [ones_at((rank == float(k)) & (count > float(k))).astype(BF16) for k in members], axis=1
        )
        span = slice(row * col_n, (row + 1) * col_n)
        placed = dot_tn(high[:, span], chosen) + dot_tn(low[:, span], chosen)
        for m in range(len(members)):
            total += placed[m * group_n : m * group_n + tracer_n, m * col_n : (m + 1) * col_n]
    burden_ref[...] = total
    copies.append(pltpu.make_async_copy(burden_ref, burden_hbm, sem.at[parts]))
    copies[-1].start()
    for copy in copies:
        copy.wait()


def local(mesh_shape, fields, neighbors, cost, dest, diffusivity, operators):
    tracer_n, level_n, row_n, col_n = fields.shape
    substep_n = operators.shape[0]
    neighbor_n = neighbors.shape[0]
    wide_n, narrow_n = mesh_shape
    dev_n = wide_n * narrow_n
    group_n = 1 << tracer_n.bit_length()
    slots = 2 * col_n // dev_n
    assert row_n == 1 and tracer_n % 4 == 0 and level_n % BAND == 0 and tracer_n * EDGES <= col_n and group_n <= col_n
    width = -(-slots * group_n // col_n) * col_n
    hbm = pl.BlockSpec(memory_space=pltpu.HBM)
    vmem = pl.BlockSpec(memory_space=pltpu.VMEM)
    chunk_n = 4
    operands = (
        fields.reshape(tracer_n, level_n, col_n),
        neighbors.reshape(neighbor_n, col_n),
        cost,
        dest,
        diffusivity.reshape(level_n, col_n),
        operators,
    )
    new, got = pl.pallas_call(
        functools.partial(kernel, wide_n, narrow_n, slots, group_n),
        out_shape=(
            jax.ShapeDtypeStruct((tracer_n, level_n, col_n), BF16),
            jax.ShapeDtypeStruct((dev_n, width), F32),
        ),
        in_specs=[hbm] * 6,
        out_specs=(vmem, vmem),
        scratch_shapes=[
            pltpu.VMEM((tracer_n, level_n, col_n), BF16),
            pltpu.VMEM((neighbor_n, col_n), I32),
            pltpu.VMEM((1, col_n), I32),
            pltpu.VMEM((1, col_n), I32),
            pltpu.VMEM((level_n, col_n), BF16),
            pltpu.VMEM((substep_n, level_n, level_n), BF16),
            pltpu.VMEM((substep_n, 2 * level_n, level_n), BF16),
            pltpu.VMEM((tracer_n, level_n, col_n), BF16),
            pltpu.VMEM((tracer_n // 2, level_n, 2 * col_n), F32),
            pltpu.VMEM((level_n, 2 * col_n), F32),
            pltpu.VMEM((level_n, col_n), BF16),
            pltpu.VMEM((2, level_n, col_n), BF16),
            pltpu.VMEM((level_n, col_n), F32),
            pltpu.VMEM((level_n, col_n), F32),
            pltpu.VMEM((level_n, col_n), BF16),
            pltpu.VMEM((level_n, col_n), F32),
            pltpu.VMEM((slots * dev_n, col_n), BF16),
            pltpu.VMEM((group_n, col_n), F32),
            pltpu.VMEM((dev_n, 1, width), F32),
            pltpu.VMEM((dev_n, 1, width), F32),
            pltpu.SemaphoreType.DMA((5,)),
            pltpu.SemaphoreType.DMA((chunk_n,)),
            pltpu.SemaphoreType.DMA((2,)),
            pltpu.SemaphoreType.DMA((2,)),
            pltpu.SemaphoreType.DMA,
            pltpu.SemaphoreType.DMA,
        ],
        compiler_params=pltpu.CompilerParams(
            collective_id=0, has_side_effects=True, vmem_limit_bytes=40 * 1024 * 1024
        ),
    )(*[pltpu.with_memory_space_constraint(value, pltpu.HBM) for value in operands])
    new, burden = pl.pallas_call(
        functools.partial(finish, slots, group_n, tracer_n),
        out_shape=(
            jax.ShapeDtypeStruct((tracer_n, level_n, col_n), BF16),
            jax.ShapeDtypeStruct((tracer_n, col_n), F32),
        ),
        in_specs=[vmem, vmem],
        out_specs=(hbm, hbm),
        scratch_shapes=[pltpu.VMEM((tracer_n, col_n), F32), pltpu.SemaphoreType.DMA((chunk_n + 1,))],
    )(*[pltpu.with_memory_space_constraint(value, pltpu.VMEM) for value in (new, got)])
    return new.reshape(fields.shape), burden[None]


def solution(mesh):
    in_specs = (
        P(None, None, "wide", "narrow"),
        P(None, "wide", "narrow"),
        P("wide", "narrow"),
        P("wide", "narrow"),
        P(None, "wide", "narrow"),
        P(),
    )
    out_specs = (P(None, None, "wide", "narrow"), P(("wide", "narrow"), None, None))
    mesh_shape = (mesh.shape["wide"], mesh.shape["narrow"])
    return jax.shard_map(
        functools.partial(local, mesh_shape),
        mesh=mesh,
        in_specs=in_specs,
        out_specs=out_specs,
        check_vma=False,
    )
```

```python
import functools

import jax
import jax.numpy as jnp
from jax import lax
from jax.experimental import pallas as pl
from jax.experimental.pallas import tpu as pltpu
from jax.sharding import PartitionSpec as P

REACH = 2
EDGES = 2 * REACH
BAND = 16
MESH = pl.DeviceIdType.MESH
F32 = jnp.float32
BF16 = jnp.bfloat16
I32 = jnp.int32


def iota(shape, dim):
    return lax.broadcasted_iota(I32, shape, dim)


def ones_at(mask):
    return jnp.where(mask, 1.0, 0.0).astype(F32)


def dot(a, b):
    return jnp.dot(a, b, preferred_element_type=F32)


def dot_nt(a, b):
    return lax.dot_general(a, b, (((1,), (1,)), ((), ())), preferred_element_type=F32)


def dot_tn(a, b):
    return lax.dot_general(a, b, (((0,), (0,)), ((), ())), preferred_element_type=F32)


def wrap(index, size):
    return jnp.where(index >= size, index - size, index)


def kernel(
    wide_n, narrow_n, slots, group_n,
    x_hbm, nb_hbm, cost_hbm, dest_hbm, diff_hbm, op_hbm,
    new_ref, got_ref,
    x_ref, nb_ref, cost_ref, dest_ref, diff_ref, op_ref,
    both_ref, dyn_ref, cur_ref, ge_ref, pack_ref, halo_ref,
    edge_ge, edge_sum, edge_dyn, edge_cur, spot_ref, sums_ref, out_slots, in_slots,
    in_sem, x_sem, halo_send, halo_recv, slot_send, slot_recv,
):
    tracer_n, level_n, col_n = x_ref.shape
    substep_n = op_ref.shape[0]
    dev_n = wide_n * narrow_n
    row_span = narrow_n * col_n
    pair_n = tracer_n // 2
    chunk_n = x_sem.shape[0]
    chunk = tracer_n // chunk_n
    wide = lax.axis_index("wide")
    narrow = lax.axis_index("narrow")
    me = wide * narrow_n + narrow
    base = narrow * col_n

    loads = []
    for index, (far, here) in enumerate(
        ((nb_hbm, nb_ref), (cost_hbm, cost_ref), (dest_hbm, dest_ref), (diff_hbm, diff_ref), (op_hbm, op_ref))
    ):
        loads.append(pltpu.make_async_copy(far, here, in_sem.at[index]))
    x_loads = []
    for index in range(chunk_n):
        part = pl.ds(index * chunk, chunk)
        x_loads.append(pltpu.make_async_copy(x_hbm.at[part], x_ref.at[part], x_sem.at[index]))
    for load in loads[:1] + loads[-1:] + x_loads + loads[1:-1]:
        load.start()

    partners = []
    for dw in range(wide_n):
        for dn in range(narrow_n):
            if dw or dn:
                partners.append((wrap(wide + dw, wide_n), wrap(narrow + dn, narrow_n)))
    barrier = pltpu.get_barrier_semaphore()
    for partner in partners:
        pl.semaphore_signal(barrier, inc=1, device_id=partner, device_id_type=MESH)

    src = iota((col_n, col_n), 0)
    lane = iota((col_n, col_n), 1)
    lane_k = lane & (EDGES - 1)
    row_k = src & (EDGES - 1)
    edge_col = jnp.where(lane_k < REACH, col_n - REACH + lane_k, lane_k - REACH)
    pick = ones_at(src == edge_col).astype(BF16)
    shift = EDGES.bit_length() - 1
    lane_q = lax.shift_right_logical(lane, shift)
    row_q = lax.shift_right_logical(src, shift)
    same_q = row_q == lane_q
    left_of = jnp.where(row_k < REACH, wrap(base + row_span - REACH + row_k, row_span), -1)
    right_of = jnp.where(row_k >= REACH, wrap(base + col_n + row_k - REACH, row_span), -1)

    loads[0].wait()
    near = ones_at(src == lane)
    from_left = jnp.zeros((col_n, col_n), F32)
    from_right = jnp.zeros((col_n, col_n), F32)
    for n in range(nb_ref.shape[0]):
        neighbor = nb_ref[n : n + 1, :]
        near += ones_at(src == neighbor - base)
        from_left += ones_at(left_of == neighbor)
        from_right += ones_at(right_of == neighbor)
    near = near.astype(BF16)

    def edge_shift(q):
        return (EDGES * q + REACH) % col_n

    for load in loads[1:]:
        load.wait()
    rows = iota((level_n, level_n), 0)
    cols = iota((level_n, level_n), 1)
    second = (
        ones_at(cols == jnp.maximum(rows - 1, 0))
        + ones_at(cols == jnp.minimum(rows + 1, level_n - 1))
        - 2.0 * ones_at(cols == rows)
    ).astype(BF16)
    for s in range(substep_n):
        curved = dot(second, op_ref[s]).astype(BF16)
        for begin in range(0, level_n, BAND):
            both_ref[s, 2 * begin : 2 * begin + BAND, :] = op_ref[s, begin : begin + BAND, :]
            both_ref[s, 2 * begin + BAND : 2 * begin + 2 * BAND, :] = curved[begin : begin + BAND]
    cost = cost_ref[...]
    gain = cost.astype(F32) / (4.0 * substep_n)
    ge = diff_ref[...].astype(F32) * gain
    ge_ref[:, :col_n] = ge
    ge_ref[:, col_n:] = ge

    edge_cost = dot(jnp.broadcast_to(cost.astype(F32), (16, col_n)).astype(BF16), pick)[:1]
    edge_ge[...] = dot(diff_ref[...], pick) * (edge_cost / (4.0 * substep_n))
    edge_left = jnp.where(same_q, dot(from_left.astype(BF16), pick), 0.0).astype(BF16)
    edge_right = jnp.where(same_q, dot(from_right.astype(BF16), pick), 0.0).astype(BF16)

    dest = dest_ref[...]
    hot = ones_at(iota((dev_n, col_n), 0) == dest)
    earlier = dot(hot.astype(BF16), ones_at(src < lane).astype(BF16))
    placed = jnp.sum(hot * earlier, axis=0, keepdims=True).astype(I32)
    spot_ref[...] = ones_at(iota((slots * dev_n, col_n), 0) == placed * dev_n + dest).astype(BF16)

    packed = jnp.zeros((level_n, col_n), F32)
    partial = jnp.zeros((level_n, col_n), F32)
    for q in range(tracer_n):
        if q % chunk == 0:
            x_loads[q // chunk].wait()
        x = x_ref[q]
        total = dot(x, near)
        packed = jnp.where(lane_q == q, pltpu.roll(x.astype(F32), edge_shift(q), 1), packed)
        partial = jnp.where(lane_q == q, pltpu.roll(total, edge_shift(q), 1), partial)
        dyn_ref[q // 2, :, (q % 2) * col_n : (q % 2 + 1) * col_n] = (0.2 * total).astype(BF16)
    pack_ref[...] = packed.astype(BF16)
    edge_sum[...] = partial

    pl.semaphore_wait(barrier, dev_n - 1)
    copies = []
    for side, step in ((0, 1), (1, narrow_n - 1)):
        copies.append(
            pltpu.make_async_remote_copy(
                src_ref=pack_ref,
                dst_ref=halo_ref.at[side],
                send_sem=halo_send.at[side],
                recv_sem=halo_recv.at[side],
                device_id=(wide, wrap(narrow + step, narrow_n)),
                device_id_type=MESH,
            )
        )
    for copy in copies:
        copy.start()

    cost_two = jnp.concatenate([cost, cost], axis=1).astype(F32)

    def advance(s, start_ref, ref, weight_ref, steps):
        now = start_ref[...] if s == 0 else ref[...].astype(BF16)
        mixed = dot(both_ref[s], now)
        for begin in range(0, level_n, BAND):
            band = slice(begin, begin + BAND)
            moved = mixed[2 * begin : 2 * begin + BAND] + weight_ref[band] * mixed[2 * begin + BAND : 2 * begin + 2 * BAND]
            ref[band] = moved if s == 0 else jnp.where(steps > float(s), moved, ref[band])

    def advance_pairs(s, pairs):
        for p in pairs:
            advance(s, dyn_ref.at[p], cur_ref.at[p], ge_ref, cost_two)

    inner_sums = []

    def add_up(q):
        change = cur_ref[q // 2, :, (q % 2) * col_n : (q % 2 + 1) * col_n] - dyn_ref[q // 2, :, (q % 2) * col_n : (q % 2 + 1) * col_n].astype(F32)
        inner_sums.append(jnp.sum(change, axis=0, keepdims=True))

    for s in range(substep_n):
        advance_pairs(s, range(pair_n // 2))

    for copy in copies:
        copy.wait()
    total = edge_sum[...] + dot(halo_ref[0], edge_left) + dot(halo_ref[1], edge_right)
    start = (0.2 * total).astype(BF16)
    edge_dyn[...] = start

    for s in range(substep_n):
        advance(s, edge_dyn, edge_cur, edge_ge, edge_cost)
        advance_pairs(s, range(pair_n // 2, pair_n))
        for q in range(s * pair_n // substep_n, (s + 1) * pair_n // substep_n):
            add_up(q)
    for q in range(pair_n, tracer_n):
        add_up(q)
    edge_end = edge_cur[...]

    col = iota((1, col_n), 1)
    inner = (col >= REACH) & (col < col_n - REACH)
    edge_start = edge_dyn[...].astype(F32)
    edge_change = edge_end - edge_start
    edge_burden = jnp.broadcast_to(jnp.sum(edge_change, axis=0, keepdims=True), (8, col_n))
    sums_ref[...] = jnp.ones(sums_ref.shape, F32)
    for q in range(tracer_n):
        outer = pltpu.roll(edge_burden, col_n - edge_shift(q), 1)[:1]
        sums_ref[q : q + 1, :] = jnp.where(inner, inner_sums[q], outer)
    per_row = col_n // group_n
    sums = sums_ref[...]
    sums = jnp.concatenate([sums] * per_row, axis=0)
    high = sums.astype(BF16)
    low = (sums - high.astype(F32)).astype(BF16)
    filled = dot_nt(spot_ref[...], high) + dot_nt(spot_ref[...], low)
    lane_group = iota((dev_n, col_n), 1) // group_n
    lines = []
    for begin in range(0, slots, per_row):
        line = jnp.zeros((dev_n, col_n), F32)
        for m in range(min(per_row, slots - begin)):
            line = jnp.where(lane_group == m, filled[(begin + m) * dev_n : (begin + m + 1) * dev_n], line)
        lines.append(line)
    line = jnp.concatenate(lines, axis=1)
    for h in range(dev_n):
        out_slots[h] = line[h : h + 1]
    in_slots[me] = out_slots[me]
    for far_wide, far_narrow in partners:
        pltpu.make_async_remote_copy(
            src_ref=out_slots.at[far_wide * narrow_n + far_narrow],
            dst_ref=in_slots.at[me],
            send_sem=slot_send,
            recv_sem=slot_recv,
            device_id=(far_wide, far_narrow),
            device_id_type=MESH,
        ).start()

    edge_new = edge_start + edge_change.astype(BF16).astype(F32)
    for q in range(tracer_n):
        dyn = dyn_ref[q // 2, :, (q % 2) * col_n : (q % 2 + 1) * col_n].astype(F32)
        change = cur_ref[q // 2, :, (q % 2) * col_n : (q % 2 + 1) * col_n] - dyn
        new = dyn + change.astype(BF16).astype(F32)
        outer = pltpu.roll(edge_new, col_n - edge_shift(q), 1)
        new_ref[q] = jnp.where(inner, new, outer).astype(BF16)

    others = pl.ds(0, dev_n - 1)
    pltpu.make_async_copy(in_slots.at[others], in_slots.at[others], slot_recv).wait()
    pltpu.make_async_copy(out_slots.at[others], out_slots.at[others], slot_send).wait()
    for h in range(dev_n):
        got_ref[h : h + 1, :] = in_slots[h]


def finish(slots, group_n, tracer_n, new_ref, got_ref, new_hbm, burden_hbm, burden_ref, sem):
    dev_n = got_ref.shape[0]
    col_n = burden_ref.shape[1]
    parts = sem.shape[0] - 1
    size = tracer_n // parts
    copies = []
    for index in range(parts):
        part = pl.ds(index * size, size)
        copies.append(pltpu.make_async_copy(new_ref.at[part], new_hbm.at[part], sem.at[index]))
    for copy in copies:
        copy.start()
    got = got_ref[...]
    width = got.shape[1]
    per_row = col_n // group_n
    flag = jnp.where(lax.rem(iota(got.shape, 1), group_n) == tracer_n, got, 0.0).astype(BF16)
    count = dot(flag, jnp.ones((width, col_n), BF16))
    before = ones_at(iota((dev_n, dev_n), 1) < iota((dev_n, dev_n), 0)).astype(BF16)
    rank = iota((dev_n, col_n), 1).astype(F32) - dot(before, count.astype(BF16))
    high = got.astype(BF16)
    low = (got - high.astype(F32)).astype(BF16)
    total = jnp.zeros((tracer_n, col_n), F32)
    for row, begin in enumerate(range(0, slots, per_row)):
        members = range(begin, min(begin + per_row, slots))
        chosen = jnp.concatenate(
            [ones_at((rank == float(k)) & (count > float(k))).astype(BF16) for k in members], axis=1
        )
        span = slice(row * col_n, (row + 1) * col_n)
        placed = dot_tn(high[:, span], chosen) + dot_tn(low[:, span], chosen)
        for m in range(len(members)):
            total += placed[m * group_n : m * group_n + tracer_n, m * col_n : (m + 1) * col_n]
    burden_ref[...] = total
    copies.append(pltpu.make_async_copy(burden_ref, burden_hbm, sem.at[parts]))
    copies[-1].start()
    for copy in copies:
        copy.wait()


def local(mesh_shape, fields, neighbors, cost, dest, diffusivity, operators):
    tracer_n, level_n, row_n, col_n = fields.shape
    substep_n = operators.shape[0]
    neighbor_n = neighbors.shape[0]
    wide_n, narrow_n = mesh_shape
    dev_n = wide_n * narrow_n
    group_n = 1 << tracer_n.bit_length()
    slots = 2 * col_n // dev_n
    assert row_n == 1 and tracer_n % 4 == 0 and level_n % BAND == 0 and tracer_n * EDGES <= col_n and group_n <= col_n
    width = -(-slots * group_n // col_n) * col_n
    hbm = pl.BlockSpec(memory_space=pltpu.HBM)
    vmem = pl.BlockSpec(memory_space=pltpu.VMEM)
    chunk_n = 4
    operands = (
        fields.reshape(tracer_n, level_n, col_n),
        neighbors.reshape(neighbor_n, col_n),
        cost,
        dest,
        diffusivity.reshape(level_n, col_n),
        operators,
    )
    new, got = pl.pallas_call(
        functools.partial(kernel, wide_n, narrow_n, slots, group_n),
        out_shape=(
            jax.ShapeDtypeStruct((tracer_n, level_n, col_n), BF16),
            jax.ShapeDtypeStruct((dev_n, width), F32),
        ),
        in_specs=[hbm] * 6,
        out_specs=(vmem, vmem),
        scratch_shapes=[
            pltpu.VMEM((tracer_n, level_n, col_n), BF16),
            pltpu.VMEM((neighbor_n, col_n), I32),
            pltpu.VMEM((1, col_n), I32),
            pltpu.VMEM((1, col_n), I32),
            pltpu.VMEM((level_n, col_n), BF16),
            pltpu.VMEM((substep_n, level_n, level_n), BF16),
            pltpu.VMEM((substep_n, 2 * level_n, level_n), BF16),
            pltpu.VMEM((tracer_n // 2, level_n, 2 * col_n), BF16),
            pltpu.VMEM((tracer_n // 2, level_n, 2 * col_n), F32),
            pltpu.VMEM((level_n, 2 * col_n), F32),
            pltpu.VMEM((level_n, col_n), BF16),
            pltpu.VMEM((2, level_n, col_n), BF16),
            pltpu.VMEM((level_n, col_n), F32),
            pltpu.VMEM((level_n, col_n), F32),
            pltpu.VMEM((level_n, col_n), BF16),
            pltpu.VMEM((level_n, col_n), F32),
            pltpu.VMEM((slots * dev_n, col_n), BF16),
            pltpu.VMEM((group_n, col_n), F32),
            pltpu.VMEM((dev_n, 1, width), F32),
            pltpu.VMEM((dev_n, 1, width), F32),
            pltpu.SemaphoreType.DMA((5,)),
            pltpu.SemaphoreType.DMA((chunk_n,)),
            pltpu.SemaphoreType.DMA((2,)),
            pltpu.SemaphoreType.DMA((2,)),
            pltpu.SemaphoreType.DMA,
            pltpu.SemaphoreType.DMA,
        ],
        compiler_params=pltpu.CompilerParams(
            collective_id=0, has_side_effects=True, vmem_limit_bytes=40 * 1024 * 1024
        ),
    )(*[pltpu.with_memory_space_constraint(value, pltpu.HBM) for value in operands])
    new, burden = pl.pallas_call(
        functools.partial(finish, slots, group_n, tracer_n),
        out_shape=(
            jax.ShapeDtypeStruct((tracer_n, level_n, col_n), BF16),
            jax.ShapeDtypeStruct((tracer_n, col_n), F32),
        ),
        in_specs=[vmem, vmem],
        out_specs=(hbm, hbm),
        scratch_shapes=[pltpu.VMEM((tracer_n, col_n), F32), pltpu.SemaphoreType.DMA((chunk_n + 1,))],
    )(*[pltpu.with_memory_space_constraint(value, pltpu.VMEM) for value in (new, got)])
    return new.reshape(fields.shape), burden[None]


def solution(mesh):
    in_specs = (
        P(None, None, "wide", "narrow"),
        P(None, "wide", "narrow"),
        P("wide", "narrow"),
        P("wide", "narrow"),
        P(None, "wide", "narrow"),
        P(),
    )
    out_specs = (P(None, None, "wide", "narrow"), P(("wide", "narrow"), None, None))
    mesh_shape = (mesh.shape["wide"], mesh.shape["narrow"])
    return jax.shard_map(
        functools.partial(local, mesh_shape),
        mesh=mesh,
        in_specs=in_specs,
        out_specs=out_specs,
        check_vma=False,
    )
```

```python
import functools

import jax
import jax.numpy as jnp
from jax import lax
from jax.experimental import pallas as pl
from jax.experimental.pallas import tpu as pltpu
from jax.sharding import PartitionSpec as P

REACH = 2
EDGES = 2 * REACH
BAND = 16
MESH = pl.DeviceIdType.MESH
F32 = jnp.float32
BF16 = jnp.bfloat16
I32 = jnp.int32


def iota(shape, dim):
    return lax.broadcasted_iota(I32, shape, dim)


def ones_at(mask):
    return jnp.where(mask, 1.0, 0.0).astype(F32)


def dot(a, b):
    return jnp.dot(a, b, preferred_element_type=F32)


def dot_nt(a, b):
    return lax.dot_general(a, b, (((1,), (1,)), ((), ())), preferred_element_type=F32)


def dot_tn(a, b):
    return lax.dot_general(a, b, (((0,), (0,)), ((), ())), preferred_element_type=F32)


def wrap(index, size):
    return jnp.where(index >= size, index - size, index)


def kernel(
    wide_n, narrow_n, slots, group_n,
    x_hbm, nb_hbm, cost_hbm, dest_hbm, diff_hbm, op_hbm,
    new_ref, got_ref,
    x_ref, nb_ref, cost_ref, dest_ref, diff_ref, op_ref,
    both_ref, dyn_ref, cur_ref, first_sum, end_sum, edge_tot, ge_ref, pack_ref, halo_ref,
    edge_ge, edge_sum, edge_dyn, edge_cur, spot_ref, sums_ref, out_slots, in_slots,
    in_sem, x_sem, halo_send, halo_recv, slot_send, slot_recv,
):
    tracer_n, level_n, col_n = x_ref.shape
    substep_n = op_ref.shape[0]
    dev_n = wide_n * narrow_n
    row_span = narrow_n * col_n
    pair_n = tracer_n // 2
    chunk_n = x_sem.shape[0]
    chunk = tracer_n // chunk_n
    wide = lax.axis_index("wide")
    narrow = lax.axis_index("narrow")
    me = wide * narrow_n + narrow
    base = narrow * col_n

    loads = []
    for index, (far, here) in enumerate(
        ((nb_hbm, nb_ref), (cost_hbm, cost_ref), (dest_hbm, dest_ref), (diff_hbm, diff_ref), (op_hbm, op_ref))
    ):
        loads.append(pltpu.make_async_copy(far, here, in_sem.at[index]))
    x_loads = []
    for index in range(chunk_n):
        part = pl.ds(index * chunk, chunk)
        x_loads.append(pltpu.make_async_copy(x_hbm.at[part], x_ref.at[part], x_sem.at[index]))
    for load in loads[:1] + x_loads + loads[1:]:
        load.start()

    partners = []
    for dw in range(wide_n):
        for dn in range(narrow_n):
            if dw or dn:
                partners.append((wrap(wide + dw, wide_n), wrap(narrow + dn, narrow_n)))
    barrier = pltpu.get_barrier_semaphore()
    for partner in partners:
        pl.semaphore_signal(barrier, inc=1, device_id=partner, device_id_type=MESH)

    src = iota((col_n, col_n), 0)
    lane = iota((col_n, col_n), 1)
    lane_k = lane & (EDGES - 1)
    row_k = src & (EDGES - 1)
    edge_col = jnp.where(lane_k < REACH, col_n - REACH + lane_k, lane_k - REACH)
    pick = ones_at(src == edge_col).astype(BF16)
    shift = EDGES.bit_length() - 1
    lane_q = lax.shift_right_logical(lane, shift)
    row_q = lax.shift_right_logical(src, shift)
    same_q = row_q == lane_q
    left_of = jnp.where(row_k < REACH, wrap(base + row_span - REACH + row_k, row_span), -1)
    right_of = jnp.where(row_k >= REACH, wrap(base + col_n + row_k - REACH, row_span), -1)

    loads[0].wait()
    near = ones_at(src == lane)
    from_left = jnp.zeros((col_n, col_n), F32)
    from_right = jnp.zeros((col_n, col_n), F32)
    for n in range(nb_ref.shape[0]):
        neighbor = nb_ref[n : n + 1, :]
        near += ones_at(src == neighbor - base)
        from_left += ones_at(left_of == neighbor)
        from_right += ones_at(right_of == neighbor)
    near = near.astype(BF16)

    def edge_shift(q):
        return (EDGES * q + REACH) % col_n

    packed = jnp.zeros((level_n, col_n), F32)
    partial = jnp.zeros((level_n, col_n), F32)
    for q in range(tracer_n):
        if q % chunk == 0:
            x_loads[q // chunk].wait()
        x = x_ref[q]
        total = dot(x, near)
        packed = jnp.where(lane_q == q, pltpu.roll(x.astype(F32), edge_shift(q), 1), packed)
        partial = jnp.where(lane_q == q, pltpu.roll(total, edge_shift(q), 1), partial)
        dyn = (0.2 * total).astype(BF16)
        half = slice((q % 2) * col_n, (q % 2 + 1) * col_n)
        dyn_ref[q // 2, :, half] = dyn
        first_sum[q // 2, :, half] = jnp.sum(dyn.astype(F32), axis=0, keepdims=True)
    pack_ref[...] = packed.astype(BF16)
    edge_sum[...] = partial

    pl.semaphore_wait(barrier, dev_n - 1)
    copies = []
    for side, step in ((0, 1), (1, narrow_n - 1)):
        copies.append(
            pltpu.make_async_remote_copy(
                src_ref=pack_ref,
                dst_ref=halo_ref.at[side],
                send_sem=halo_send.at[side],
                recv_sem=halo_recv.at[side],
                device_id=(wide, wrap(narrow + step, narrow_n)),
                device_id_type=MESH,
            )
        )
    for copy in copies:
        copy.start()

    for load in loads[1:]:
        load.wait()
    rows = iota((level_n, level_n), 0)
    cols = iota((level_n, level_n), 1)
    second = (
        ones_at(cols == jnp.maximum(rows - 1, 0))
        + ones_at(cols == jnp.minimum(rows + 1, level_n - 1))
        - 2.0 * ones_at(cols == rows)
    ).astype(BF16)
    for s in range(substep_n):
        curved = dot(second, op_ref[s]).astype(BF16)
        for begin in range(0, level_n, BAND):
            both_ref[s, 2 * begin : 2 * begin + BAND, :] = op_ref[s, begin : begin + BAND, :]
            both_ref[s, 2 * begin + BAND : 2 * begin + 2 * BAND, :] = curved[begin : begin + BAND]
    cost = cost_ref[...]
    gain = cost.astype(F32) / (4.0 * substep_n)
    ge = diff_ref[...].astype(F32) * gain
    ge_ref[:, :col_n] = ge
    ge_ref[:, col_n:] = ge

    edge_cost = dot(jnp.broadcast_to(cost.astype(F32), (16, col_n)).astype(BF16), pick)[:1]
    edge_ge[...] = dot(diff_ref[...], pick) * (edge_cost / (4.0 * substep_n))
    edge_left = jnp.where(same_q, dot(from_left.astype(BF16), pick), 0.0).astype(BF16)
    edge_right = jnp.where(same_q, dot(from_right.astype(BF16), pick), 0.0).astype(BF16)

    dest = dest_ref[...]
    hot = ones_at(iota((dev_n, col_n), 0) == dest)
    earlier = dot(hot.astype(BF16), ones_at(src < lane).astype(BF16))
    placed = jnp.sum(hot * earlier, axis=0, keepdims=True).astype(I32)
    spot_ref[...] = ones_at(iota((slots * dev_n, col_n), 0) == placed * dev_n + dest).astype(BF16)

    cost_two = jnp.concatenate([cost, cost], axis=1).astype(F32)

    def advance(s, start_ref, ref, sum_ref, weight_ref, steps):
        now = start_ref[...] if s == 0 else ref[...]
        mixed = dot(both_ref[s], now)
        live = jnp.broadcast_to(steps.astype(BF16), (BAND, steps.shape[1])) > jnp.asarray(s, BF16)
        added = jnp.zeros((BAND, steps.shape[1]), F32)
        for begin in range(0, level_n, BAND):
            band = slice(begin, begin + BAND)
            moved = mixed[2 * begin : 2 * begin + BAND] + weight_ref[band] * mixed[2 * begin + BAND : 2 * begin + 2 * BAND]
            added += moved
            rounded = moved.astype(BF16)
            ref[band] = rounded if s == 0 else jnp.where(live, rounded, now[band])
        added = jnp.sum(added, axis=0, keepdims=True)
        sum_ref[...] = added if s == 0 else jnp.where(steps > float(s), added, sum_ref[...])

    def advance_pairs(s, pairs):
        for p in pairs:
            advance(s, dyn_ref.at[p], cur_ref.at[p], end_sum.at[p], ge_ref, cost_two)

    for s in range(substep_n):
        advance_pairs(s, range(pair_n // 2))

    for copy in copies:
        copy.wait()
    total = edge_sum[...] + dot(halo_ref[0], edge_left) + dot(halo_ref[1], edge_right)
    start = (0.2 * total).astype(BF16)
    edge_dyn[...] = start

    for s in range(substep_n):
        advance(s, edge_dyn, edge_cur, edge_tot, edge_ge, edge_cost)
        advance_pairs(s, range(pair_n // 2, pair_n))

    col = iota((1, col_n), 1)
    inner = (col >= REACH) & (col < col_n - REACH)
    edge_start = edge_dyn[...].astype(F32)
    edge_change = edge_cur[...].astype(F32) - edge_start
    edge_burden = jnp.broadcast_to(
        edge_tot[...] - jnp.sum(edge_start, axis=0, keepdims=True), (8, col_n)
    )
    sums_ref[...] = jnp.ones(sums_ref.shape, F32)
    for q in range(tracer_n):
        outer = pltpu.roll(edge_burden, col_n - edge_shift(q), 1)[:1]
        half = slice((q % 2) * col_n, (q % 2 + 1) * col_n)
        own = end_sum[q // 2, :, half] - first_sum[q // 2, :, half]
        sums_ref[q : q + 1, :] = jnp.where(inner, own, outer)
    per_row = col_n // group_n
    sums = sums_ref[...]
    sums = jnp.concatenate([sums] * per_row, axis=0)
    high = sums.astype(BF16)
    low = (sums - high.astype(F32)).astype(BF16)
    filled = dot_nt(spot_ref[...], high) + dot_nt(spot_ref[...], low)
    lane_group = iota((dev_n, col_n), 1) // group_n
    lines = []
    for begin in range(0, slots, per_row):
        line = jnp.zeros((dev_n, col_n), F32)
        for m in range(min(per_row, slots - begin)):
            line = jnp.where(lane_group == m, filled[(begin + m) * dev_n : (begin + m + 1) * dev_n], line)
        lines.append(line)
    line = jnp.concatenate(lines, axis=1)
    for h in range(dev_n):
        out_slots[h] = line[h : h + 1]
    in_slots[me] = out_slots[me]
    for far_wide, far_narrow in partners:
        pltpu.make_async_remote_copy(
            src_ref=out_slots.at[far_wide * narrow_n + far_narrow],
            dst_ref=in_slots.at[me],
            send_sem=slot_send,
            recv_sem=slot_recv,
            device_id=(far_wide, far_narrow),
            device_id_type=MESH,
        ).start()

    edge_new = edge_start + edge_change.astype(BF16).astype(F32)
    for q in range(tracer_n):
        dyn = dyn_ref[q // 2, :, (q % 2) * col_n : (q % 2 + 1) * col_n].astype(F32)
        change = cur_ref[q // 2, :, (q % 2) * col_n : (q % 2 + 1) * col_n].astype(F32) - dyn
        new = dyn + change.astype(BF16).astype(F32)
        outer = pltpu.roll(edge_new, col_n - edge_shift(q), 1)
        new_ref[q] = jnp.where(inner, new, outer).astype(BF16)

    others = pl.ds(0, dev_n - 1)
    pltpu.make_async_copy(in_slots.at[others], in_slots.at[others], slot_recv).wait()
    pltpu.make_async_copy(out_slots.at[others], out_slots.at[others], slot_send).wait()
    for h in range(dev_n):
        got_ref[h : h + 1, :] = in_slots[h]


def finish(slots, group_n, tracer_n, new_ref, got_ref, new_hbm, burden_hbm, burden_ref, sem):
    dev_n = got_ref.shape[0]
    col_n = burden_ref.shape[1]
    parts = sem.shape[0] - 1
    size = tracer_n // parts
    copies = []
    for index in range(parts):
        part = pl.ds(index * size, size)
        copies.append(pltpu.make_async_copy(new_ref.at[part], new_hbm.at[part], sem.at[index]))
    for copy in copies:
        copy.start()
    got = got_ref[...]
    width = got.shape[1]
    per_row = col_n // group_n
    flag = jnp.where(lax.rem(iota(got.shape, 1), group_n) == tracer_n, got, 0.0).astype(BF16)
    count = dot(flag, jnp.ones((width, col_n), BF16))
    before = ones_at(iota((dev_n, dev_n), 1) < iota((dev_n, dev_n), 0)).astype(BF16)
    rank = iota((dev_n, col_n), 1).astype(F32) - dot(before, count.astype(BF16))
    high = got.astype(BF16)
    low = (got - high.astype(F32)).astype(BF16)
    total = jnp.zeros((tracer_n, col_n), F32)
    for row, begin in enumerate(range(0, slots, per_row)):
        members = range(begin, min(begin + per_row, slots))
        chosen = jnp.concatenate(
            [ones_at((rank == float(k)) & (count > float(k))).astype(BF16) for k in members], axis=1
        )
        span = slice(row * col_n, (row + 1) * col_n)
        placed = dot_tn(high[:, span], chosen) + dot_tn(low[:, span], chosen)
        for m in range(len(members)):
            total += placed[m * group_n : m * group_n + tracer_n, m * col_n : (m + 1) * col_n]
    burden_ref[...] = total
    copies.append(pltpu.make_async_copy(burden_ref, burden_hbm, sem.at[parts]))
    copies[-1].start()
    for copy in copies:
        copy.wait()


def local(mesh_shape, fields, neighbors, cost, dest, diffusivity, operators):
    tracer_n, level_n, row_n, col_n = fields.shape
    substep_n = operators.shape[0]
    neighbor_n = neighbors.shape[0]
    wide_n, narrow_n = mesh_shape
    dev_n = wide_n * narrow_n
    group_n = 1 << tracer_n.bit_length()
    slots = 2 * col_n // dev_n
    assert row_n == 1 and tracer_n % 4 == 0 and level_n % BAND == 0 and tracer_n * EDGES <= col_n and group_n <= col_n
    width = -(-slots * group_n // col_n) * col_n
    hbm = pl.BlockSpec(memory_space=pltpu.HBM)
    vmem = pl.BlockSpec(memory_space=pltpu.VMEM)
    chunk_n = 4
    operands = (
        fields.reshape(tracer_n, level_n, col_n),
        neighbors.reshape(neighbor_n, col_n),
        cost,
        dest,
        diffusivity.reshape(level_n, col_n),
        operators,
    )
    new, got = pl.pallas_call(
        functools.partial(kernel, wide_n, narrow_n, slots, group_n),
        out_shape=(
            jax.ShapeDtypeStruct((tracer_n, level_n, col_n), BF16),
            jax.ShapeDtypeStruct((dev_n, width), F32),
        ),
        in_specs=[hbm] * 6,
        out_specs=(vmem, vmem),
        scratch_shapes=[
            pltpu.VMEM((tracer_n, level_n, col_n), BF16),
            pltpu.VMEM((neighbor_n, col_n), I32),
            pltpu.VMEM((1, col_n), I32),
            pltpu.VMEM((1, col_n), I32),
            pltpu.VMEM((level_n, col_n), BF16),
            pltpu.VMEM((substep_n, level_n, level_n), BF16),
            pltpu.VMEM((substep_n, 2 * level_n, level_n), BF16),
            pltpu.VMEM((tracer_n // 2, level_n, 2 * col_n), BF16),
            pltpu.VMEM((tracer_n // 2, level_n, 2 * col_n), BF16),
            pltpu.VMEM((tracer_n // 2, 1, 2 * col_n), F32),
            pltpu.VMEM((tracer_n // 2, 1, 2 * col_n), F32),
            pltpu.VMEM((1, col_n), F32),
            pltpu.VMEM((level_n, 2 * col_n), F32),
            pltpu.VMEM((level_n, col_n), BF16),
            pltpu.VMEM((2, level_n, col_n), BF16),
            pltpu.VMEM((level_n, col_n), F32),
            pltpu.VMEM((level_n, col_n), F32),
            pltpu.VMEM((level_n, col_n), BF16),
            pltpu.VMEM((level_n, col_n), BF16),
            pltpu.VMEM((slots * dev_n, col_n), BF16),
            pltpu.VMEM((group_n, col_n), F32),
            pltpu.VMEM((dev_n, 1, width), F32),
            pltpu.VMEM((dev_n, 1, width), F32),
            pltpu.SemaphoreType.DMA((5,)),
            pltpu.SemaphoreType.DMA((chunk_n,)),
            pltpu.SemaphoreType.DMA((2,)),
            pltpu.SemaphoreType.DMA((2,)),
            pltpu.SemaphoreType.DMA,
            pltpu.SemaphoreType.DMA,
        ],
        compiler_params=pltpu.CompilerParams(
            collective_id=0, has_side_effects=True, vmem_limit_bytes=40 * 1024 * 1024
        ),
    )(*[pltpu.with_memory_space_constraint(value, pltpu.HBM) for value in operands])
    new, burden = pl.pallas_call(
        functools.partial(finish, slots, group_n, tracer_n),
        out_shape=(
            jax.ShapeDtypeStruct((tracer_n, level_n, col_n), BF16),
            jax.ShapeDtypeStruct((tracer_n, col_n), F32),
        ),
        in_specs=[vmem, vmem],
        out_specs=(hbm, hbm),
        scratch_shapes=[pltpu.VMEM((tracer_n, col_n), F32), pltpu.SemaphoreType.DMA((chunk_n + 1,))],
    )(*[pltpu.with_memory_space_constraint(value, pltpu.VMEM) for value in (new, got)])
    return new.reshape(fields.shape), burden[None]


def solution(mesh):
    in_specs = (
        P(None, None, "wide", "narrow"),
        P(None, "wide", "narrow"),
        P("wide", "narrow"),
        P("wide", "narrow"),
        P(None, "wide", "narrow"),
        P(),
    )
    out_specs = (P(None, None, "wide", "narrow"), P(("wide", "narrow"), None, None))
    mesh_shape = (mesh.shape["wide"], mesh.shape["narrow"])
    return jax.shard_map(
        functools.partial(local, mesh_shape),
        mesh=mesh,
        in_specs=in_specs,
        out_specs=out_specs,
        check_vma=False,
    )
```
